32 devices in a mesh: row: 8 (over z, x), col: 4 (over y, core).
Axes of the slice: x: 2, y: 2, z: 4, core: 2. Of those that a mesh axis runs over, the one named last changes fastest.
Arguments:
- southeast_edges: bfloat16 [8, 4, 2, 2, 2, 96, 768], P('row', 'col'), may hold values from -6 to 6
- northwest_edges: bfloat16 [8, 4, 2, 2, 2, 96, 768], P('row', 'col'), may hold values from -6 to 6
- southeast_corners: bfloat16 [8, 4, 2, 2, 96, 128], P('row', 'col'), may hold values from -6 to 6
- northwest_corners: bfloat16 [8, 4, 2, 2, 96, 128], P('row', 'col'), may hold values from -6 to 6
- operators: bfloat16 [8, 4, 2, 2, 768, 768], P('row', 'col'), may hold values from -0.109375 to 0.109375
- sources: bfloat16 [8, 4, 2, 2, 96, 768], P('row', 'col'), may hold values from -3 to 3
- roster: int32 [2, 3, 2], replicated, may hold values from 0 to 1, as said below
Outputs:
- southeast_out: bfloat16 [8, 4, 2, 2, 2, 96, 768], P('row', 'col')
- northwest_out: bfloat16 [8, 4, 2, 2, 2, 96, 768], P('row', 'col')
- southeast_corner_out: bfloat16 [8, 4, 2, 2, 96, 128], P('row', 'col')
- northwest_corner_out: bfloat16 [8, 4, 2, 2, 96, 128], P('row', 'col')
The draws below stay inside these ranges and needn't reach their ends.
Inputs may be any that keep to these rules, and one draw needn't show every extreme that they name: roster[d, k, b] is the class, modulo 2, of the antidiagonals on which batch b of direction d stands at tick k. It rises by one modulo 2 from each tick to the next, and at every tick the 2 batches of one direction take all classes, each once.
All inputs are finite; a program needn't handle non-finite values.
Results may differ from the reference program's by a relative error of at most 0.0051.
Values may be sent and summed in bfloat16 or wider, within the bound.
No kernel may reach another device: no remote copies, remote signals or barrier semaphores. Data moves between devices by JAX's collectives and lax.ppermute only.
A program may use at most 64 MiB of HBM per device.

```python
import jax
import jax.numpy as jnp
from jax import lax

EDGE = 768
CORNER = 128
SHOTS = 96
BATCHES = 2
TICKS = 3
NR = 8
NC = 4


def draw_roster(key, part):
    ticks_column = jnp.arange(TICKS, dtype=jnp.int32)[:, None]
    planes = []
    for direction in range(2):
        subkey = jax.random.fold_in(key, 17 + direction)
        start = jax.random.randint(jax.random.fold_in(subkey, 1), (), 0, BATCHES).astype(jnp.int32)
        order = jax.random.permutation(jax.random.fold_in(subkey, 2), BATCHES).astype(jnp.int32)
        planes.append(jnp.mod(order[None, :] + start + ticks_column, BATCHES).astype(jnp.int32))
    return jnp.stack(planes).astype(jnp.int32)


def block_levels(own_key, extent, cuts, smallest, top_value):
    def one(position, parts):
        steps = jax.random.uniform(jax.random.fold_in(jax.random.fold_in(own_key, 6), position), (parts,), jnp.float32, smallest / len(cuts), top_value / len(cuts))
        return jnp.repeat(jnp.exp(steps), extent[position] // parts).reshape((-1,) + (1,) * (len(extent) - position - 1))

    factor_of = one(*cuts[0])
    for cut in cuts[1:]:
        factor_of = factor_of * one(*cut)
    return factor_of


def bell_draw(own_key, shape, width, most, split=(), kind=jnp.bfloat16):
    array = width * jax.random.normal(own_key, shape, jnp.float32)
    if split:
        array = array * block_levels(own_key, shape, split, -0.22, 0.18)
    return jnp.clip(array, -most, most).astype(kind)


def setup_inputs(seed: int = 0) -> dict:
    keys = jax.random.split(jax.random.key(seed), 8)
    southeast_edges = bell_draw(keys[0], (NR, NC, 2, BATCHES, 2, SHOTS, EDGE), 1.0, 6.0, ((0, 8), (1, 4)))
    northwest_edges = bell_draw(keys[1], (NR, NC, 2, BATCHES, 2, SHOTS, EDGE), 1.0, 6.0, ((0, 8), (1, 4)))
    southeast_corners = bell_draw(keys[2], (NR, NC, BATCHES, 2, SHOTS, CORNER), 1.0, 6.0, ((0, 8), (1, 4)))
    northwest_corners = bell_draw(keys[3], (NR, NC, BATCHES, 2, SHOTS, CORNER), 1.0, 6.0, ((0, 8), (1, 4)))
    operators = bell_draw(keys[4], (NR, NC, 2, 2, EDGE, EDGE), (4 * EDGE) ** -0.5, 0.109375, ((0, 8), (1, 4)))
    sources = bell_draw(keys[5], (NR, NC, BATCHES, 2, SHOTS, EDGE), 0.5, 3.0, ((0, 8), (1, 4)))
    roster = draw_roster(jax.random.fold_in(keys[7], 71), 0)
    return dict(southeast_edges=southeast_edges, northwest_edges=northwest_edges, southeast_corners=southeast_corners, northwest_corners=northwest_corners, operators=operators, sources=sources, roster=roster)


def trace_update(first_in, second_in, corner_in, cell_operators, source, flipped):
    shot_count = first_in.shape[1]
    edge_width = first_in.shape[2]
    corner_width = corner_in.shape[-1]
    stacked = jnp.stack([first_in, second_in]).reshape(4 * shot_count, edge_width).astype(jnp.float32)
    form = "qe,mpfe->mpqf" if flipped else "qe,mpef->mpqf"
    products = jnp.einsum(form, stacked, cell_operators.astype(jnp.float32), precision=lax.Precision.HIGHEST)
    products = products.reshape(2, 2, 2, 2, shot_count, edge_width)

    def complex_product(source_index, operator_index):
        real_part = products[operator_index, 0, source_index, 0] - products[operator_index, 1, source_index, 1]
        imag_part = products[operator_index, 1, source_index, 0] + products[operator_index, 0, source_index, 1]
        return jnp.stack([real_part, imag_part])

    source_value = source.astype(jnp.float32)
    corner_value = corner_in.astype(jnp.float32)
    first_out = complex_product(0, 0) + complex_product(1, 1) + source_value
    second_out = complex_product(0, 1) + complex_product(1, 0) + source_value
    if flipped:
        first_out = first_out.at[:, :, edge_width - corner_width:].add(corner_value)
        second_out = second_out.at[:, :, edge_width - corner_width:].add(corner_value)
        corner_out = 0.5 * (first_out[:, :, :corner_width] + second_out[:, :, :corner_width])
    else:
        first_out = first_out.at[:, :, :corner_width].add(corner_value)
        second_out = second_out.at[:, :, :corner_width].add(corner_value)
        corner_out = 0.5 * (first_out[:, :, edge_width - corner_width:] + second_out[:, :, edge_width - corner_width:])
    return first_out.astype(jnp.bfloat16), second_out.astype(jnp.bfloat16), corner_out.astype(jnp.bfloat16)


def sweep_tick(states, corner_states, operators, sources, plan, flipped):
    cell_numbers = jnp.arange(NR * NC, dtype=jnp.int32)
    row_numbers = (cell_numbers // NC).astype(jnp.int32)
    col_numbers = (cell_numbers % NC).astype(jnp.int32)
    offset = 1 if flipped else -1

    def one_cell(packed):
        row_index, col_index = packed
        if flipped:
            klass = jnp.mod((NR - 1 - row_index) + (NC - 1 - col_index), BATCHES)
        else:
            klass = jnp.mod(row_index + col_index, BATCHES)
        batch_index = jnp.argmax((plan == klass).astype(jnp.int32)).astype(jnp.int32)
        near_row = jnp.mod(row_index + offset, NR).astype(jnp.int32)
        near_col = jnp.mod(col_index + offset, NC).astype(jnp.int32)
        first_in = states[near_row, col_index, 0, batch_index]
        second_in = states[row_index, near_col, 1, batch_index]
        corner_in = corner_states[near_row, near_col, batch_index]
        first_out, second_out, corner_out = trace_update(first_in, second_in, corner_in,
                                                         operators[row_index, col_index],
                                                         sources[row_index, col_index, batch_index], flipped)
        return first_out, second_out, corner_out, batch_index

    firsts, seconds, corner_outs, batch_list = lax.map(one_cell, (row_numbers, col_numbers))
    renewed = states.at[row_numbers, col_numbers, 0, batch_list].set(firsts)
    renewed = renewed.at[row_numbers, col_numbers, 1, batch_list].set(seconds)
    renewed_corners = corner_states.at[row_numbers, col_numbers, batch_list].set(corner_outs)
    return renewed, renewed_corners


def reference(southeast_edges, northwest_edges, southeast_corners, northwest_corners, operators, sources, roster):
    down_states, up_states = southeast_edges, northwest_edges
    down_corners, up_corners = southeast_corners, northwest_corners
    for tick_index in range(TICKS):
        down_states, down_corners = sweep_tick(down_states, down_corners, operators, sources,
                                               roster[0, tick_index], False)
        up_states, up_corners = sweep_tick(up_states, up_corners, operators, sources,
                                           roster[1, tick_index], True)
    return down_states, up_states, down_corners, up_corners
```

```python
import functools

import jax
import jax.numpy as jnp
from jax import lax
from jax.experimental import pallas as pl
from jax.experimental.pallas import tpu as pltpu
from jax.sharding import PartitionSpec as P

ANY = pl.BlockSpec(memory_space=pl.ANY)
VMEM = pl.BlockSpec(memory_space=pltpu.VMEM)
SMEM = pl.BlockSpec(memory_space=pltpu.SMEM)
VMEM_LIMIT = 40 * 1024 * 1024


def chosen_at_start(roster_ref, direction, row_count, col_count):
    row = lax.axis_index("row")
    col = lax.axis_index("col")
    if direction:
        row = row_count - 1 - row
        col = col_count - 1 - col
    klass = lax.rem(row + col, 2)
    return jnp.where(roster_ref[direction, 0, 0] == klass, 0, 1)


def run_copies(copies):
    for copy in copies:
        copy.start()
    for copy in copies:
        copy.wait()


def select_kernel(
    counts, roster, se_edges, nw_edges, se_corners, nw_corners, *refs
):
    outs, sems = refs[:6], refs[6]
    copies = []
    for direction, (edges, corners) in enumerate(
        ((se_edges, se_corners), (nw_edges, nw_corners))
    ):
        mine = chosen_at_start(roster, direction, *counts)
        other = 1 - mine
        by_row, by_col, by_diagonal = outs[3 * direction : 3 * direction + 3]
        edge_width = edges.shape[-1]
        corner_width = corners.shape[-1]
        pairs = (
            (edges.at[0, other], by_row),
            (edges.at[1, other], by_col.at[:, :, pl.ds(0, edge_width)]),
            (corners.at[other], by_col.at[:, :, pl.ds(edge_width, corner_width)]),
            (corners.at[mine], by_diagonal),
        )
        for index, (source, target) in enumerate(pairs):
            copies.append(
                pltpu.make_async_copy(source, target, sems.at[direction, index])
            )
    run_copies(copies)


def select_initial(counts, roster, se_edges, nw_edges, se_corners, nw_corners):
    _, _, parts, shots, edge_width = se_edges.shape
    corner_width = se_corners.shape[-1]
    kind = se_edges.dtype
    shapes = [
        jax.ShapeDtypeStruct((parts, shots, edge_width), kind),
        jax.ShapeDtypeStruct((parts, shots, edge_width + corner_width), kind),
        jax.ShapeDtypeStruct((parts, shots, corner_width), kind),
    ] * 2
    return pl.pallas_call(
        functools.partial(select_kernel, counts),
        out_shape=shapes,
        in_specs=[SMEM] + [ANY] * 4,
        out_specs=[ANY] * 6,
        scratch_shapes=[pltpu.SemaphoreType.DMA((2, 4))],
        name="select_initial",
    )(roster, se_edges, nw_edges, se_corners, nw_corners)


def load_kernel(operators, plain, flipped, sems):
    count = operators.shape[0]
    edge_width = operators.shape[1]
    copies = [
        pltpu.make_async_copy(
            operators.at[i], plain.at[pl.ds(i * edge_width, edge_width)], sems.at[i]
        )
        for i in range(count)
    ]
    for copy in copies:
        copy.start()
    for i in range(count):
        copies[i].wait()
        rows = pl.ds(i * edge_width, edge_width)
        flipped[rows, :] = plain[rows, :].T


def load_operators(operators):
    count = operators.shape[0] * operators.shape[1]
    edge_width = operators.shape[-1]
    shape = (count * edge_width, edge_width)
    return pl.pallas_call(
        load_kernel,
        out_shape=[pltpu.VMEM(shape, operators.dtype), pltpu.VMEM(shape, operators.dtype)],
        in_specs=[ANY],
        out_specs=[VMEM, VMEM],
        scratch_shapes=[pltpu.SemaphoreType.DMA((count,))],
        compiler_params=pltpu.CompilerParams(vmem_limit_bytes=VMEM_LIMIT),
        name="load_operators",
    )(operators.reshape(count, edge_width, edge_width))


def tick_kernel(
    counts, direction, tick, last, edge_width, corner_width, roster, first_in, second_in,
    corner_in, sources, operators, *refs
):
    if last:
        old_first, old_second, old_corner, edges_out, corners_out = refs[:5]
        refs = refs[5:]
    else:
        first_out, second_out, corner_out = refs[:3]
        refs = refs[3:]
    first_v, second_v, corner_v, source_v, left, first_o, second_o, corner_o, sems = refs
    parts, shots, _ = source_v.shape
    rows = parts * shots
    chosen = chosen_at_start(roster, direction, *counts)
    if tick % 2:
        chosen = 1 - chosen
    edge_part = pl.ds(0, edge_width)
    corner_part = pl.ds(edge_width, corner_width)

    first_copy = pltpu.make_async_copy(first_in, first_v, sems.at[0])
    second_copy = pltpu.make_async_copy(second_in, second_v, sems.at[1])
    source_copy = pltpu.make_async_copy(sources.at[chosen], source_v, sems.at[2])
    inputs = [first_copy, second_copy, source_copy]
    if tick == 0:
        corner_copy = pltpu.make_async_copy(corner_in, corner_v, sems.at[3])
        inputs.append(corner_copy)
    for copy in inputs:
        copy.start()
    history = []
    if last:
        history = [
            pltpu.make_async_copy(
                old_first.at[:, :, edge_part], edges_out.at[0, 1 - chosen], sems.at[4]
            ),
            pltpu.make_async_copy(
                old_second.at[:, :, edge_part], edges_out.at[1, 1 - chosen], sems.at[5]
            ),
            pltpu.make_async_copy(old_corner, corners_out.at[1 - chosen], sems.at[6]),
        ]
        for copy in history:
            copy.start()
    for copy in inputs:
        copy.wait()

    for place, ref in ((0, first_v), (2, second_v)):
        other_place = 2 - place
        real = ref[0, :, edge_part]
        imag = ref[1, :, edge_part]
        minus = -imag
        for slot, block in ((place, 0), (other_place, 1)):
            row = block * rows
            column = slot * edge_width
            left[pl.ds(row, shots), pl.ds(column, edge_width)] = real
            left[pl.ds(row + shots, shots), pl.ds(column, edge_width)] = imag
            left[pl.ds(row, shots), pl.ds(column + edge_width, edge_width)] = minus
            left[pl.ds(row + shots, shots), pl.ds(column + edge_width, edge_width)] = real

    if tick == 0:
        corner = corner_v[...]
    else:
        corner = first_v[:, :, corner_part]
    corner = corner.astype(jnp.float32).reshape(rows, corner_width)
    if not last and first_o.shape[-1] > edge_width:
        first_o[:, :, corner_part] = second_v[:, :, corner_part]

    tile = edge_width // 3 if edge_width % 3 == 0 else edge_width
    steps = edge_width // tile
    for step in range(steps):
        at = pl.ds(step * tile, tile)
        value = jnp.dot(left[...], operators[:, at], preferred_element_type=jnp.float32)
        source = source_v[:, :, at].astype(jnp.float32).reshape(rows, tile)
        first = value[:rows] + source
        second = value[rows:] + source
        low, high = step == 0, step == steps - 1
        adds, gives = (high, low) if direction else (low, high)

        def at_corner(array, flag):
            if flag:
                return array[:, tile - corner_width :]
            return array[:, :corner_width]

        if adds:
            widths = ((0, 0), (tile - corner_width, 0) if direction else (0, tile - corner_width))
            padded = jnp.pad(corner, widths)
            first = first + padded
            second = second + padded
        if gives:
            value = 0.5 * (at_corner(first, not direction) + at_corner(second, not direction))
            value = value.astype(corner_o.dtype).reshape(parts, shots, corner_width)
            corner_o[...] = value
            if not last and second_o.shape[-1] > edge_width:
                second_o[:, :, corner_part] = value
        first_o[:, :, at] = first.astype(first_o.dtype).reshape(parts, shots, tile)
        second_o[:, :, at] = second.astype(second_o.dtype).reshape(parts, shots, tile)

    if last:
        copies = [
            pltpu.make_async_copy(first_o, edges_out.at[0, chosen], sems.at[7]),
            pltpu.make_async_copy(second_o, edges_out.at[1, chosen], sems.at[8]),
            pltpu.make_async_copy(corner_o, corners_out.at[chosen], sems.at[9]),
        ]
    else:
        copies = [
            pltpu.make_async_copy(first_o, first_out, sems.at[7]),
            pltpu.make_async_copy(second_o, second_out, sems.at[8]),
            pltpu.make_async_copy(corner_o, corner_out, sems.at[9]),
        ]
    run_copies(copies)
    for copy in history:
        copy.wait()


def tick_update(
    counts, direction, tick, ticks, roster, first_in, second_in, corner_in, sources, operators,
    history,
):
    batches, parts, shots, edge_width = sources.shape
    corner_width = corner_in.shape[-1]
    kind = sources.dtype
    last = tick == ticks - 1
    first_width = edge_width + (0 if last else corner_width)
    second_width = edge_width + (0 if tick >= ticks - 2 else corner_width)
    shapes = [
        jax.ShapeDtypeStruct((parts, shots, first_width), kind),
        jax.ShapeDtypeStruct((parts, shots, second_width), kind),
        jax.ShapeDtypeStruct((parts, shots, corner_width), kind),
    ]
    if last:
        outs = [
            jax.ShapeDtypeStruct((2, batches, parts, shots, edge_width), kind),
            jax.ShapeDtypeStruct((batches, parts, shots, corner_width), kind),
        ]
    else:
        outs = shapes
    operands = [roster, first_in, second_in, corner_in, sources, operators]
    if last:
        operands += list(history)
    rows = parts * shots
    return pl.pallas_call(
        functools.partial(tick_kernel, counts, direction, tick, last, edge_width, corner_width),
        out_shape=outs,
        in_specs=[SMEM, ANY, ANY, ANY, ANY, VMEM] + [ANY] * (len(operands) - 6),
        out_specs=[ANY] * len(outs),
        scratch_shapes=[
            pltpu.VMEM(first_in.shape, kind),
            pltpu.VMEM(second_in.shape, kind),
            pltpu.VMEM((parts, shots, corner_width), kind),
            pltpu.VMEM((parts, shots, edge_width), kind),
            pltpu.VMEM((2 * rows, 4 * edge_width), kind),
            pltpu.VMEM(shapes[0].shape, kind),
            pltpu.VMEM(shapes[1].shape, kind),
            pltpu.VMEM(shapes[2].shape, kind),
            pltpu.SemaphoreType.DMA((10,)),
        ],
        compiler_params=pltpu.CompilerParams(vmem_limit_bytes=VMEM_LIMIT),
        cost_estimate=pl.CostEstimate(
            flops=2 * 2 * rows * 4 * edge_width * edge_width,
            bytes_accessed=6 * rows * edge_width * 2,
            transcendentals=0,
        ),
        name="tick" + str(tick) + ("nw" if direction else "se"),
    )(*operands)


def neighbours(counts, row_step, col_step):
    row_count, col_count = counts
    return [
        (r * col_count + c, (r + row_step) % row_count * col_count + (c + col_step) % col_count)
        for r in range(row_count)
        for c in range(col_count)
    ]


def move(array, counts, row_step, col_step):
    return lax.ppermute(array, ("row", "col"), neighbours(counts, row_step, col_step))


def shards(
    southeast_edges, northwest_edges, southeast_corners, northwest_corners, operators, sources,
    roster,
):
    counts = (lax.axis_size("row"), lax.axis_size("col"))
    ticks = roster.shape[1]
    local_sources = sources[0, 0]
    picked = select_initial(
        counts, roster, southeast_edges[0, 0], northwest_edges[0, 0], southeast_corners[0, 0],
        northwest_corners[0, 0],
    )
    prepared = load_operators(operators[0, 0])
    sends = [picked[:3], picked[3:]]
    history = [None, None]
    outs = [None, None]
    corners = [None, None]
    for tick in range(ticks):
        arrived = []
        for direction in range(2):
            by = -1 if direction else 1
            first, second, corner = sends[direction]
            first_in = move(first, counts, by, 0)
            second_in = move(second, counts, 0, by)
            if tick == 0:
                corners[direction] = move(corner, counts, by, by)
            arrived.append((first_in, second_in))
        for direction in range(2):
            first_in, second_in = arrived[direction]
            done = tick_update(
                counts, direction, tick, ticks, roster, first_in, second_in, corners[direction],
                local_sources, prepared[direction], history[direction],
            )
            if tick == ticks - 1:
                outs[direction] = done
            else:
                sends[direction] = done
                history[direction] = done
    return (
        outs[0][0][None, None],
        outs[1][0][None, None],
        outs[0][1][None, None],
        outs[1][1][None, None],
    )


def solution(mesh):
    edges = P("row", "col", None, None, None, None, None)
    corners = P("row", "col", None, None, None, None)
    return jax.shard_map(
        shards,
        mesh=mesh,
        in_specs=(edges, edges, corners, corners, corners, corners, P()),
        out_specs=(edges, edges, corners, corners),
        check_vma=False,
    )
```

```python
import functools

import jax
import jax.numpy as jnp
from jax import lax
from jax.experimental import pallas as pl
from jax.experimental.pallas import tpu as pltpu
from jax.sharding import PartitionSpec as P

ANY = pl.BlockSpec(memory_space=pl.ANY)
VMEM = pl.BlockSpec(memory_space=pltpu.VMEM)
SMEM = pl.BlockSpec(memory_space=pltpu.SMEM)
HBM = pl.BlockSpec(memory_space=pltpu.HBM)
VMEM_LIMIT = 40 * 1024 * 1024


def chosen_at_start(roster_ref, direction, row_count, col_count):
    row = lax.axis_index("row")
    col = lax.axis_index("col")
    if direction:
        row = row_count - 1 - row
        col = col_count - 1 - col
    klass = lax.rem(row + col, 2)
    return jnp.where(roster_ref[direction, 0, 0] == klass, 0, 1)


def in_hbm(array):
    return pltpu.with_memory_space_constraint(array, pltpu.HBM)


def run_copies(copies):
    for copy in copies:
        copy.start()
    for copy in copies:
        copy.wait()


def select_kernel(
    counts, roster, se_edges, nw_edges, se_corners, nw_corners, *refs
):
    outs, sems = refs[:6], refs[6]
    copies = []
    for direction, (edges, corners) in enumerate(
        ((se_edges, se_corners), (nw_edges, nw_corners))
    ):
        mine = chosen_at_start(roster, direction, *counts)
        other = 1 - mine
        by_row, by_col, by_diagonal = outs[3 * direction : 3 * direction + 3]
        edge_width = edges.shape[-1]
        corner_width = corners.shape[-1]
        pairs = (
            (edges.at[0, other], by_row),
            (edges.at[1, other], by_col.at[:, :, pl.ds(0, edge_width)]),
            (corners.at[other], by_col.at[:, :, pl.ds(edge_width, corner_width)]),
            (corners.at[mine], by_diagonal),
        )
        for index, (source, target) in enumerate(pairs):
            copies.append(
                pltpu.make_async_copy(source, target, sems.at[direction, index])
            )
    run_copies(copies)


def select_initial(counts, roster, se_edges, nw_edges, se_corners, nw_corners):
    _, _, parts, shots, edge_width = se_edges.shape
    corner_width = se_corners.shape[-1]
    kind = se_edges.dtype
    shapes = [
        pltpu.VMEM((parts, shots, edge_width), kind),
        pltpu.VMEM((parts, shots, edge_width + corner_width), kind),
        pltpu.VMEM((parts, shots, corner_width), kind),
    ] * 2
    return pl.pallas_call(
        functools.partial(select_kernel, counts),
        out_shape=shapes,
        in_specs=[SMEM] + [HBM] * 4,
        out_specs=[VMEM] * 6,
        scratch_shapes=[pltpu.SemaphoreType.DMA((2, 4))],
        compiler_params=pltpu.CompilerParams(vmem_limit_bytes=VMEM_LIMIT),
        name="select_initial",
    )(roster, *map(in_hbm, (se_edges, nw_edges, se_corners, nw_corners)))


def load_kernel(operators, plain, flipped, sems):
    count = operators.shape[0]
    edge_width = operators.shape[1]
    copies = [
        pltpu.make_async_copy(
            operators.at[i], plain.at[pl.ds(i * edge_width, edge_width)], sems.at[i]
        )
        for i in range(count)
    ]
    for copy in copies:
        copy.start()
    for i in range(count):
        copies[i].wait()
        rows = pl.ds(i * edge_width, edge_width)
        flipped[rows, :] = plain[rows, :].T


def load_operators(operators):
    count = operators.shape[0] * operators.shape[1]
    edge_width = operators.shape[-1]
    shape = (count * edge_width, edge_width)
    return pl.pallas_call(
        load_kernel,
        out_shape=[pltpu.VMEM(shape, operators.dtype), pltpu.VMEM(shape, operators.dtype)],
        in_specs=[HBM],
        out_specs=[VMEM, VMEM],
        scratch_shapes=[pltpu.SemaphoreType.DMA((count,))],
        compiler_params=pltpu.CompilerParams(vmem_limit_bytes=VMEM_LIMIT),
        name="load_operators",
    )(in_hbm(operators.reshape(count, edge_width, edge_width)))


def tick_kernel(
    counts, direction, tick, last, edge_width, corner_width, roster, first_in, second_in,
    corner_in, sources, operators, *refs
):
    if last:
        old_first, old_second, old_corner, edges_out, corners_out = refs[:5]
        left, first_out, second_out, corner_out, sems = refs[5:]
    else:
        first_out, second_out, corner_out, left = refs
    parts, shots = sources.shape[1:3]
    rows = parts * shots
    chosen = chosen_at_start(roster, direction, *counts)
    if tick % 2:
        chosen = 1 - chosen
    edge_part = pl.ds(0, edge_width)
    corner_part = pl.ds(edge_width, corner_width)

    history = []
    if last:
        history = [
            pltpu.make_async_copy(
                old_first.at[:, :, edge_part], edges_out.at[0, 1 - chosen], sems.at[0]
            ),
            pltpu.make_async_copy(
                old_second.at[:, :, edge_part], edges_out.at[1, 1 - chosen], sems.at[1]
            ),
            pltpu.make_async_copy(old_corner, corners_out.at[1 - chosen], sems.at[2]),
        ]
        for copy in history:
            copy.start()

    for place, ref in ((0, first_in), (2, second_in)):
        other_place = 2 - place
        real = ref[0, :, edge_part]
        imag = ref[1, :, edge_part]
        minus = -imag
        for slot, block in ((place, 0), (other_place, 1)):
            row = block * rows
            column = slot * edge_width
            left[pl.ds(row, shots), pl.ds(column, edge_width)] = real
            left[pl.ds(row + shots, shots), pl.ds(column, edge_width)] = imag
            left[pl.ds(row, shots), pl.ds(column + edge_width, edge_width)] = minus
            left[pl.ds(row + shots, shots), pl.ds(column + edge_width, edge_width)] = real

    corner = corner_in[...] if tick == 0 else first_in[:, :, corner_part]
    corner = corner.astype(jnp.float32).reshape(rows, corner_width)
    if first_out.shape[-1] > edge_width:
        first_out[:, :, corner_part] = second_in[:, :, corner_part]

    tile = edge_width // 3 if edge_width % 3 == 0 else edge_width
    steps = edge_width // tile
    for step in range(steps):
        at = pl.ds(step * tile, tile)
        value = jnp.dot(left[...], operators[:, at], preferred_element_type=jnp.float32)
        source = sources[chosen, :, :, at].astype(jnp.float32).reshape(rows, tile)
        first = value[:rows] + source
        second = value[rows:] + source
        low, high = step == 0, step == steps - 1
        adds, gives = (high, low) if direction else (low, high)

        def at_corner(array, flag):
            if flag:
                return array[:, tile - corner_width :]
            return array[:, :corner_width]

        if adds:
            widths = ((0, 0), (tile - corner_width, 0) if direction else (0, tile - corner_width))
            padded = jnp.pad(corner, widths)
            first = first + padded
            second = second + padded
        if gives:
            value = 0.5 * (at_corner(first, not direction) + at_corner(second, not direction))
            value = value.astype(corner_out.dtype).reshape(parts, shots, corner_width)
            corner_out[...] = value
            if second_out.shape[-1] > edge_width:
                second_out[:, :, corner_part] = value
        first_out[:, :, at] = first.astype(first_out.dtype).reshape(parts, shots, tile)
        second_out[:, :, at] = second.astype(second_out.dtype).reshape(parts, shots, tile)

    if last:
        run_copies(
            [
                pltpu.make_async_copy(first_out, edges_out.at[0, chosen], sems.at[3]),
                pltpu.make_async_copy(second_out, edges_out.at[1, chosen], sems.at[4]),
                pltpu.make_async_copy(corner_out, corners_out.at[chosen], sems.at[5]),
            ]
        )
    for copy in history:
        copy.wait()


def tick_update(
    counts, direction, tick, ticks, roster, first_in, second_in, corner_in, sources, operators,
    history,
):
    batches, parts, shots, edge_width = sources.shape
    corner_width = corner_in.shape[-1]
    kind = sources.dtype
    last = tick == ticks - 1
    first_width = edge_width + (0 if last else corner_width)
    second_width = edge_width + (0 if tick >= ticks - 2 else corner_width)
    rows = parts * shots
    shapes = [
        pltpu.VMEM((parts, shots, first_width), kind),
        pltpu.VMEM((parts, shots, second_width), kind),
        pltpu.VMEM((parts, shots, corner_width), kind),
    ]
    scratch = [pltpu.VMEM((2 * rows, 4 * edge_width), kind)]
    operands = [roster, first_in, second_in, corner_in, sources, operators]
    in_specs = [SMEM] + [VMEM] * 5
    if last:
        outs = [
            jax.ShapeDtypeStruct((2, batches, parts, shots, edge_width), kind),
            jax.ShapeDtypeStruct((batches, parts, shots, corner_width), kind),
        ]
        out_specs = [HBM] * 2
        scratch += shapes + [pltpu.SemaphoreType.DMA((6,))]
        operands += list(history)
        in_specs += [VMEM] * 3
    else:
        outs = shapes
        out_specs = [VMEM] * 3
    return pl.pallas_call(
        functools.partial(tick_kernel, counts, direction, tick, last, edge_width, corner_width),
        out_shape=outs,
        in_specs=in_specs,
        out_specs=out_specs,
        scratch_shapes=scratch,
        compiler_params=pltpu.CompilerParams(vmem_limit_bytes=VMEM_LIMIT),
        cost_estimate=pl.CostEstimate(
            flops=2 * 2 * rows * 4 * edge_width * edge_width,
            bytes_accessed=6 * rows * edge_width * 2,
            transcendentals=0,
        ),
        name="tick" + str(tick) + ("nw" if direction else "se"),
    )(*operands)


def neighbours(counts, row_step, col_step):
    row_count, col_count = counts
    return [
        (r * col_count + c, (r + row_step) % row_count * col_count + (c + col_step) % col_count)
        for r in range(row_count)
        for c in range(col_count)
    ]


def move(array, counts, row_step, col_step):
    return lax.ppermute(array, ("row", "col"), neighbours(counts, row_step, col_step))


def shards(
    southeast_edges, northwest_edges, southeast_corners, northwest_corners, operators, sources,
    roster,
):
    counts = (lax.axis_size("row"), lax.axis_size("col"))
    ticks = roster.shape[1]
    roster = roster.transpose(0, 2, 1)
    local_sources = sources[0, 0]
    picked = select_initial(
        counts, roster, southeast_edges[0, 0], northwest_edges[0, 0], southeast_corners[0, 0],
        northwest_corners[0, 0],
    )
    prepared = load_operators(operators[0, 0])
    sends = [picked[:3], picked[3:]]
    history = [None, None]
    outs = [None, None]
    corners = [None, None]
    for tick in range(ticks):
        arrived = []
        for direction in range(2):
            by = -1 if direction else 1
            first, second, corner = sends[direction]
            first_in = move(first, counts, by, 0)
            second_in = move(second, counts, 0, by)
            if tick == 0:
                corners[direction] = move(corner, counts, by, by)
            arrived.append((first_in, second_in))
        for direction in range(2):
            first_in, second_in = arrived[direction]
            done = tick_update(
                counts, direction, tick, ticks, roster, first_in, second_in, corners[direction],
                local_sources, prepared[direction], history[direction],
            )
            if tick == ticks - 1:
                outs[direction] = done
            else:
                sends[direction] = done
                history[direction] = done
    return (
        outs[0][0][None, None],
        outs[1][0][None, None],
        outs[0][1][None, None],
        outs[1][1][None, None],
    )


def solution(mesh):
    edges = P("row", "col", None, None, None, None, None)
    corners = P("row", "col", None, None, None, None)
    return jax.shard_map(
        shards,
        mesh=mesh,
        in_specs=(edges, edges, corners, corners, corners, corners, P()),
        out_specs=(edges, edges, corners, corners),
        check_vma=False,
    )
```

```python
import functools

import jax
import jax.numpy as jnp
from jax import lax
from jax.experimental import pallas as pl
from jax.experimental.pallas import tpu as pltpu
from jax.sharding import PartitionSpec as P

VMEM = pl.BlockSpec(memory_space=pltpu.VMEM)
SMEM = pl.BlockSpec(memory_space=pltpu.SMEM)
HBM = pl.BlockSpec(memory_space=pltpu.HBM)
VMEM_LIMIT = 40 * 1024 * 1024


def direction_at(row, col, tick, stream):
    return (row + col + tick + 1 + stream) % 2


def in_hbm(array):
    return pltpu.with_memory_space_constraint(array, pltpu.HBM)


def own_direction(tick, stream):
    return direction_at(lax.axis_index("row"), lax.axis_index("col"), tick, stream)


def chosen_at_start(roster_ref, direction, counts):
    row = lax.axis_index("row")
    col = lax.axis_index("col")
    if direction:
        row = counts[0] - 1 - row
        col = counts[1] - 1 - col
    klass = lax.rem(row + col, 2)
    return jnp.where(roster_ref[direction, 0, 0] == klass, 0, 1)


def start(copy):
    copy.start()


def wait(copy):
    copy.wait()


def select_slots(counts, stream, roster, edges, corners, outs, sems, act):
    by_row, by_col, by_diagonal = outs
    edge_width = by_row.shape[-1]
    corner_width = by_diagonal.shape[-1]
    for going in range(2):

        @pl.when(own_direction(-1, stream) == going)
        def _():
            other = 1 - chosen_at_start(roster, going, counts)
            own = going if False else 1 - going
            mine = chosen_at_start(roster, own, counts)
            pairs = (
                (edges[going].at[0, other], by_row),
                (corners[own].at[mine], by_diagonal),
                (edges[going].at[1, other], by_col.at[:, :, pl.ds(0, edge_width)]),
                (corners[going].at[other], by_col.at[:, :, pl.ds(edge_width, corner_width)]),
            )
            for index, (source, target) in enumerate(pairs):
                act(pltpu.make_async_copy(source, target, sems.at[index]))


def select_kernel(counts, stream, roster, se_edges, nw_edges, se_corners, nw_corners, *refs):
    outs, sems = refs[:3], refs[3]
    for act in (start, wait):
        select_slots(
            counts, stream, roster, (se_edges, nw_edges), (se_corners, nw_corners), outs, sems, act
        )


def slot_shapes(edges, corners):
    _, _, parts, shots, edge_width = edges.shape
    corner_width = corners.shape[-1]
    return [
        pltpu.VMEM((parts, shots, edge_width), edges.dtype),
        pltpu.VMEM((parts, shots, edge_width + corner_width), edges.dtype),
        pltpu.VMEM((parts, shots, corner_width), edges.dtype),
    ]


def select_initial(counts, stream, roster, states):
    return pl.pallas_call(
        functools.partial(select_kernel, counts, stream),
        out_shape=slot_shapes(states[0], states[2]),
        in_specs=[SMEM] + [HBM] * 4,
        out_specs=[VMEM] * 3,
        scratch_shapes=[pltpu.SemaphoreType.DMA((4,))],
        compiler_params=pltpu.CompilerParams(vmem_limit_bytes=VMEM_LIMIT),
        name="select_initial",
    )(roster, *map(in_hbm, states))


def load_kernel(
    counts, stream, roster, se_edges, nw_edges, se_corners, nw_corners, operators, sources, *refs
):
    outs = refs[:3]
    prepared, picked, select_sems, operator_sems, source_sems = refs[3:]
    count, edge_width, _ = operators.shape
    copies = [
        pltpu.make_async_copy(
            operators.at[i],
            prepared.at[0, pl.ds(i * edge_width, edge_width)],
            operator_sems.at[i],
        )
        for i in range(count)
    ]
    source_copies = []
    for direction in range(2):
        mine = chosen_at_start(roster, direction, counts)
        for late in range(2):
            source_copies.append(
                pltpu.make_async_copy(
                    sources.at[1 - mine if late else mine],
                    picked.at[direction, late],
                    source_sems.at[direction, late],
                )
            )
    edges, corners = (se_edges, nw_edges), (se_corners, nw_corners)
    for copy in copies:
        copy.start()
    select_slots(counts, stream, roster, edges, corners, outs, select_sems, start)
    for copy in source_copies:
        copy.start()
    for i in range(count):
        copies[i].wait()
        rows = pl.ds(i * edge_width, edge_width)
        prepared[1, rows, :] = prepared[0, rows, :].T
    select_slots(counts, stream, roster, edges, corners, outs, select_sems, wait)
    for copy in source_copies:
        copy.wait()


def load_operators(counts, stream, roster, states, operators, sources):
    count = operators.shape[0] * operators.shape[1]
    edge_width = operators.shape[-1]
    kind = operators.dtype
    operators = operators.reshape(count, edge_width, edge_width)
    return pl.pallas_call(
        functools.partial(load_kernel, counts, stream),
        out_shape=slot_shapes(states[0], states[2])
        + [
            pltpu.VMEM((2, count * edge_width, edge_width), kind),
            pltpu.VMEM((2,) + sources.shape, kind),
        ],
        in_specs=[SMEM] + [HBM] * 6,
        out_specs=[VMEM] * 5,
        scratch_shapes=[
            pltpu.SemaphoreType.DMA((4,)),
            pltpu.SemaphoreType.DMA((count,)),
            pltpu.SemaphoreType.DMA((2, 2)),
        ],
        compiler_params=pltpu.CompilerParams(vmem_limit_bytes=VMEM_LIMIT),
        cost_estimate=cost(False),
        name="load_operators",
    )(roster, *map(in_hbm, states), in_hbm(operators), in_hbm(sources))


def compute(
    tick, stream, corner_width, first_in, second_in, corner_in, sources, operators, outs, left, act
):
    first_out, second_out, *corner_out = outs
    parts, shots, edge_width = sources.shape[2:]
    rows = parts * shots
    direction = own_direction(tick, stream)
    edge_part = pl.ds(0, edge_width)
    corner_part = pl.ds(edge_width, corner_width)

    for place, ref in ((0, first_in), (2, second_in)):
        other_place = 2 - place
        real = ref[0, :, edge_part]
        imag = ref[1, :, edge_part]
        minus = -imag
        for slot, block in ((place, 0), (other_place, 1)):
            row = block * rows
            column = slot * edge_width
            left[pl.ds(row, shots), pl.ds(column, edge_width)] = real
            left[pl.ds(row + shots, shots), pl.ds(column, edge_width)] = imag
            left[pl.ds(row, shots), pl.ds(column + edge_width, edge_width)] = minus
            left[pl.ds(row + shots, shots), pl.ds(column + edge_width, edge_width)] = real

    corner = corner_in[...] if tick == 0 else first_in[:, :, corner_part]
    corner = corner.astype(jnp.float32).reshape(rows, corner_width)
    if first_out.shape[-1] > edge_width:
        first_out[:, :, corner_part] = second_in[:, :, corner_part]

    tile = edge_width // 3 if edge_width % 3 == 0 else edge_width
    steps = edge_width // tile
    for step in range(steps):
        at = pl.ds(step * tile, tile)
        value = jnp.dot(left[...], operators[direction, :, at], preferred_element_type=jnp.float32)
        source = sources[direction, tick % 2, :, :, at].astype(jnp.float32).reshape(rows, tile)
        first = value[:rows] + source
        second = value[rows:] + source
        for end in range(2):
            if step != (steps - 1 if end else 0):
                continue
            here = slice(tile - corner_width, tile) if end else slice(0, corner_width)
            added = jnp.where(direction == end, corner, 0.0)
            widths = ((0, 0), (tile - corner_width, 0) if end else (0, tile - corner_width))
            added = jnp.pad(added, widths)
            first = first + added
            second = second + added
            given = (0.5 * (first[:, here] + second[:, here])).astype(second_out.dtype)
            given = given.reshape(parts, shots, corner_width)

            @pl.when(direction != end)
            def _():
                for ref in corner_out:
                    ref[...] = given
                if second_out.shape[-1] > edge_width:
                    second_out[:, :, corner_part] = given

        first_out[:, :, at] = first.astype(first_out.dtype).reshape(parts, shots, tile)
        second_out[:, :, at] = second.astype(second_out.dtype).reshape(parts, shots, tile)
        act(step, at)


def middle_kernel(
    tick, stream, corner_width, first_in, second_in, corner_in, sources, operators, *refs
):
    outs, left = refs[:-1], refs[-1]
    compute(
        tick, stream, corner_width, first_in, second_in, corner_in, sources, operators, outs, left,
        lambda step, at: None,
    )


def last_kernel(
    counts, tick, stream, histories, corner_width, roster, first_in, second_in, sources, operators,
    *refs
):
    count = len(histories)
    older = [refs[3 * i : 3 * i + 3] for i in range(count)]
    refs = refs[3 * count :]
    if not count:
        refs = refs[4:]
    edges_out, corners_out, (left, *outs, old_sems, sems) = refs[0:2], refs[2:4], refs[4:]
    edge_width = sources.shape[-1]
    edge_part = pl.ds(0, edge_width)

    def each(at_tick, at_stream, act_on):
        for direction in range(2):

            @pl.when(own_direction(at_tick, at_stream) == direction)
            def _():
                batch = chosen_at_start(roster, direction, counts)
                if at_tick % 2:
                    batch = 1 - batch
                act_on(edges_out[direction], corners_out[direction], batch)

    def old_stores(index, act):
        first, second, corner = older[index]

        def act_on(edges, corners, batch):
            pairs = (
                (first.at[:, :, edge_part], edges.at[0, batch]),
                (second.at[:, :, edge_part], edges.at[1, batch]),
                (corner, corners.at[batch]),
            )
            for place, (source, target) in enumerate(pairs):
                act(pltpu.make_async_copy(source, target, old_sems.at[index, place]))

        each(tick - 1, histories[index], act_on)

    def tile_store(act, step, at):
        def act_on(edges, corners, batch):
            for slot in range(2):
                act(
                    pltpu.make_async_copy(
                        outs[slot].at[:, :, at], edges.at[slot, batch, :, :, at],
                        sems.at[slot, step],
                    )
                )

        each(tick, stream, act_on)

    def corner_store(act):
        each(
            tick, stream,
            lambda edges, corners, batch: act(
                pltpu.make_async_copy(outs[2], corners.at[batch], sems.at[2, 0])
            ),
        )

    for index in range(count):
        old_stores(index, start)
    tiles = []

    def stored(step, at):
        tiles.append((step, at))
        tile_store(start, step, at)

    compute(
        tick, stream, corner_width, first_in, second_in, None, sources, operators, outs, left,
        stored,
    )
    corner_store(start)
    for index in range(count):
        old_stores(index, wait)
    for step, at in tiles:
        tile_store(wait, step, at)
    corner_store(wait)


def tick_shapes(sources, corner_width, tick, ticks):
    _, _, parts, shots, edge_width = sources.shape
    kind = sources.dtype
    first_width = edge_width + (0 if tick == ticks - 1 else corner_width)
    second_width = edge_width + (0 if tick >= ticks - 2 else corner_width)
    shapes = [
        pltpu.VMEM((parts, shots, first_width), kind),
        pltpu.VMEM((parts, shots, second_width), kind),
    ]
    if tick >= ticks - 2:
        shapes.append(pltpu.VMEM((parts, shots, corner_width), kind))
    return shapes


def cost(heavy):
    return pl.CostEstimate(flops=10**10 if heavy else 0, bytes_accessed=1, transcendentals=0)


def left_side(sources):
    _, _, parts, shots, edge_width = sources.shape
    return pltpu.VMEM((2 * parts * shots, 4 * edge_width), sources.dtype)


def middle_tick(tick, ticks, stream, first_in, second_in, corner_in, sources, operators):
    shapes = tick_shapes(sources, corner_in.shape[-1], tick, ticks)
    return pl.pallas_call(
        functools.partial(middle_kernel, tick, stream, corner_in.shape[-1]),
        out_shape=shapes,
        in_specs=[VMEM] * 5,
        out_specs=[VMEM] * len(shapes),
        scratch_shapes=[left_side(sources)],
        compiler_params=pltpu.CompilerParams(vmem_limit_bytes=VMEM_LIMIT),
        cost_estimate=cost(tick == 0 and stream == 0),
        name="tick" + str(tick) + "_stream" + str(stream),
    )(first_in, second_in, corner_in, sources, operators)


def last_tick(
    counts, tick, ticks, stream, roster, first_in, second_in, sources, operators, history, so_far,
    corner_width,
):
    _, batches, parts, shots, edge_width = sources.shape
    kind = sources.dtype
    outs = [jax.ShapeDtypeStruct((2, batches, parts, shots, edge_width), kind)] * 2
    outs += [jax.ShapeDtypeStruct((batches, parts, shots, corner_width), kind)] * 2
    operands = [roster, first_in, second_in, sources, operators]
    in_specs = [SMEM] + [VMEM] * 4
    aliases = {}
    if so_far is None:
        for traces in history:
            operands += list(traces)
        in_specs += [VMEM] * 6
        histories = (0, 1)
    else:
        aliases = {len(operands) + i: i for i in range(4)}
        operands += list(so_far)
        in_specs += [HBM] * 4
        histories = ()
    return pl.pallas_call(
        functools.partial(last_kernel, counts, tick, stream, histories, corner_width),
        out_shape=outs,
        in_specs=in_specs,
        out_specs=[HBM] * 4,
        scratch_shapes=[left_side(sources)]
        + tick_shapes(sources, corner_width, tick, ticks)
        + [pltpu.SemaphoreType.DMA((2, 3)), pltpu.SemaphoreType.DMA((3, 3))],
        input_output_aliases=aliases,
        compiler_params=pltpu.CompilerParams(vmem_limit_bytes=VMEM_LIMIT),
        cost_estimate=cost(False),
        name="tick" + str(tick) + "_stream" + str(stream),
    )(*operands)


def move(array, counts, step_of_cell):
    row_count, col_count = counts
    pairs = []
    for row in range(row_count):
        for col in range(col_count):
            down, right = step_of_cell(row, col)
            to_row = (row + down) % row_count
            to_col = (col + right) % col_count
            pairs.append((row * col_count + col, to_row * col_count + to_col))
    return lax.ppermute(array, ("row", "col"), pairs)


def sense(row, col, tick, stream):
    return -1 if direction_at(row, col, tick, stream) else 1


def by_row(array, counts, tick, stream):
    return move(array, counts, lambda row, col: (sense(row, col, tick - 1, stream), 0))


def by_col(array, counts, tick, stream):
    return move(array, counts, lambda row, col: (0, sense(row, col, tick - 1, stream)))


def by_diagonal(array, counts, stream):
    return move(array, counts, lambda row, col: (sense(row, col, 0, stream),) * 2)


def shards(
    southeast_edges, northwest_edges, southeast_corners, northwest_corners, operators, sources,
    roster,
):
    counts = (lax.axis_size("row"), lax.axis_size("col"))
    ticks = roster.shape[1]
    corner_width = southeast_corners.shape[-1]
    roster = roster.transpose(0, 2, 1)
    states = (
        southeast_edges[0, 0], northwest_edges[0, 0], southeast_corners[0, 0],
        northwest_corners[0, 0],
    )
    slots = [select_initial(counts, 0, roster, states), None]
    *rest, prepared, picked = load_operators(
        counts, 1, roster, states, operators[0, 0], sources[0, 0]
    )
    slots[1] = rest
    corners = [None, None]
    firsts = [slots[stream][0] for stream in range(2)]
    seconds = [slots[stream][1] for stream in range(2)]
    outs = None
    for tick in range(ticks):
        done = []
        for stream in range(2):
            second_in = by_col(seconds[stream], counts, tick, stream)
            if tick == 0:
                corners[stream] = by_diagonal(slots[stream][2], counts, stream)
            first_in = by_row(firsts[stream], counts, tick, stream)
            if tick < ticks - 1:
                done.append(
                    middle_tick(
                        tick, ticks, stream, first_in, second_in, corners[stream], picked, prepared
                    )
                )
            else:
                outs = last_tick(
                    counts, tick, ticks, stream, roster, first_in, second_in, picked, prepared,
                    history, outs, corner_width,
                )
        if tick < ticks - 1:
            history = done
            firsts = [done[0][0], done[1][0]]
            seconds = [done[0][1], done[1][1]]
    return tuple(array[None, None] for array in outs)


def solution(mesh):
    edges = P("row", "col", None, None, None, None, None)
    corners = P("row", "col", None, None, None, None)
    return jax.shard_map(
        shards,
        mesh=mesh,
        in_specs=(edges, edges, corners, corners, corners, corners, P()),
        out_specs=(edges, edges, corners, corners),
        check_vma=False,
    )
```

```python
import functools

import jax
import jax.numpy as jnp
from jax import lax
from jax.experimental import pallas as pl
from jax.experimental.pallas import tpu as pltpu
from jax.sharding import PartitionSpec as P

VMEM = pl.BlockSpec(memory_space=pltpu.VMEM)
SMEM = pl.BlockSpec(memory_space=pltpu.SMEM)
HBM = pl.BlockSpec(memory_space=pltpu.HBM)
VMEM_LIMIT = 40 * 1024 * 1024


def direction_at(row, col, tick, stream):
    return (row + col + tick + 1 + stream) % 2


def in_hbm(array):
    return pltpu.with_memory_space_constraint(array, pltpu.HBM)


def own_direction(tick, stream):
    return direction_at(lax.axis_index("row"), lax.axis_index("col"), tick, stream)


def chosen_at_start(roster_ref, direction, counts):
    row = lax.axis_index("row")
    col = lax.axis_index("col")
    if direction:
        row = counts[0] - 1 - row
        col = counts[1] - 1 - col
    klass = lax.rem(row + col, 2)
    return jnp.where(roster_ref[direction, 0, 0] == klass, 0, 1)


def start(copy):
    copy.start()


def wait(copy):
    copy.wait()


def select_slots(counts, stream, roster, edges, corners, outs, sems, act):
    by_row, by_col, by_diagonal = outs
    edge_width = by_row.shape[-1]
    corner_width = by_diagonal.shape[-1]
    for going in range(2):

        @pl.when(own_direction(-1, stream) == going)
        def _():
            other = 1 - chosen_at_start(roster, going, counts)
            own = going if False else 1 - going
            mine = chosen_at_start(roster, own, counts)
            pairs = (
                (edges[going].at[0, other], by_row),
                (corners[own].at[mine], by_diagonal),
                (edges[going].at[1, other], by_col.at[:, :, pl.ds(0, edge_width)]),
                (corners[going].at[other], by_col.at[:, :, pl.ds(edge_width, corner_width)]),
            )
            for index, (source, target) in enumerate(pairs):
                act(pltpu.make_async_copy(source, target, sems.at[index]))


def select_kernel(
    counts, stream, roster, se_edges, nw_edges, se_corners, nw_corners, by_row, by_col, by_diagonal,
    numbers, all_edges, all_corners, sems
):
    edges, corners = (se_edges, nw_edges), (se_corners, nw_corners)
    edge_width = by_row.shape[-1]
    corner_width = by_diagonal.shape[-1]
    roster_copy = pltpu.make_async_copy(roster, numbers, sems.at[0])
    roster_copy.start()
    own = 1 - own_direction(-1, stream)

    def fetch(act):
        for going in range(2):

            @pl.when(own_direction(-1, stream) == going)
            def _():
                act(pltpu.make_async_copy(edges[going], all_edges, sems.at[1]))

            act(pltpu.make_async_copy(corners[going], all_corners.at[going], sems.at[2 + going]))

    fetch(start)
    roster_copy.wait()
    chosen = [chosen_at_start(numbers, direction, counts) for direction in range(2)]
    other = 1 - jnp.where(own == 0, chosen[1], chosen[0])
    mine = jnp.where(own == 0, chosen[0], chosen[1])
    fetch(wait)
    by_row[...] = all_edges[0, other]
    by_col[:, :, pl.ds(0, edge_width)] = all_edges[1, other]
    by_col[:, :, pl.ds(edge_width, corner_width)] = all_corners[1 - own, other]
    by_diagonal[...] = all_corners[own, mine]


def slot_shapes(edges, corners):
    _, _, parts, shots, edge_width = edges.shape
    corner_width = corners.shape[-1]
    return [
        pltpu.VMEM((parts, shots, edge_width), edges.dtype),
        pltpu.VMEM((parts, shots, edge_width + corner_width), edges.dtype),
        pltpu.VMEM((parts, shots, corner_width), edges.dtype),
    ]


def select_initial(counts, stream, roster, states):
    edges, _, corners, _ = states
    return pl.pallas_call(
        functools.partial(select_kernel, counts, stream),
        out_shape=slot_shapes(edges, corners),
        in_specs=[HBM] * 5,
        out_specs=[VMEM] * 3,
        scratch_shapes=[
            pltpu.SMEM(roster.shape, roster.dtype),
            pltpu.VMEM(edges.shape, edges.dtype),
            pltpu.VMEM((2,) + corners.shape, corners.dtype),
            pltpu.SemaphoreType.DMA((4,)),
        ],
        compiler_params=pltpu.CompilerParams(vmem_limit_bytes=VMEM_LIMIT),
        name="select_initial",
    )(roster, *map(in_hbm, states))


def load_kernel(
    counts, stream, roster, se_edges, nw_edges, se_corners, nw_corners, operators, sources, *refs
):
    outs = refs[:3]
    prepared, picked, flags, select_sems, operator_sems, source_sems = refs[3:]
    count, edge_width, _ = operators.shape
    copies = [
        pltpu.make_async_copy(
            operators.at[i],
            prepared.at[0, pl.ds(i * edge_width, edge_width)],
            operator_sems.at[i],
        )
        for i in range(count)
    ]
    source_copies = []
    for direction in range(2):
        mine = chosen_at_start(roster, direction, counts)
        flags[direction] = jnp.full(flags.shape[1:], mine.astype(jnp.float32))
        for late in range(2):
            source_copies.append(
                pltpu.make_async_copy(
                    sources.at[1 - mine if late else mine],
                    picked.at[direction, late],
                    source_sems.at[direction, late],
                )
            )
    edges, corners = (se_edges, nw_edges), (se_corners, nw_corners)
    for copy in copies:
        copy.start()
    select_slots(counts, stream, roster, edges, corners, outs, select_sems, start)
    for copy in source_copies:
        copy.start()
    for i in range(count):
        copies[i].wait()
        rows = pl.ds(i * edge_width, edge_width)
        prepared[1, rows, :] = prepared[0, rows, :].T
    select_slots(counts, stream, roster, edges, corners, outs, select_sems, wait)
    for copy in source_copies:
        copy.wait()


def load_operators(counts, stream, roster, states, operators, sources):
    count = operators.shape[0] * operators.shape[1]
    edge_width = operators.shape[-1]
    kind = operators.dtype
    operators = operators.reshape(count, edge_width, edge_width)
    return pl.pallas_call(
        functools.partial(load_kernel, counts, stream),
        out_shape=slot_shapes(states[0], states[2])
        + [
            pltpu.VMEM((2, count * edge_width, edge_width), kind),
            pltpu.VMEM((2,) + sources.shape, kind),
            pltpu.VMEM((2, 8, 128), jnp.float32),
        ],
        in_specs=[SMEM] + [HBM] * 6,
        out_specs=[VMEM] * 6,
        scratch_shapes=[
            pltpu.SemaphoreType.DMA((4,)),
            pltpu.SemaphoreType.DMA((count,)),
            pltpu.SemaphoreType.DMA((2, 2)),
        ],
        compiler_params=pltpu.CompilerParams(vmem_limit_bytes=VMEM_LIMIT),
        cost_estimate=cost(False),
        name="load_operators",
    )(roster, *map(in_hbm, states), in_hbm(operators), in_hbm(sources))


def compute(
    tick, stream, corner_width, first_in, second_in, corner_in, sources, operators, outs, left, act
):
    first_out, second_out = outs
    parts, shots, edge_width = sources.shape[2:]
    rows = parts * shots
    direction = own_direction(tick, stream)
    edge_part = pl.ds(0, edge_width)
    corner_part = pl.ds(edge_width, corner_width)

    for place, ref in ((0, first_in), (2, second_in)):
        other_place = 2 - place
        real = ref[0, :, edge_part]
        imag = ref[1, :, edge_part]
        minus = -imag
        for slot, block in ((place, 0), (other_place, 1)):
            row = block * rows
            column = slot * edge_width
            left[pl.ds(row, shots), pl.ds(column, edge_width)] = real
            left[pl.ds(row + shots, shots), pl.ds(column, edge_width)] = imag
            left[pl.ds(row, shots), pl.ds(column + edge_width, edge_width)] = minus
            left[pl.ds(row + shots, shots), pl.ds(column + edge_width, edge_width)] = real

    corner = corner_in[...] if tick == 0 else first_in[:, :, corner_part]
    corner = corner.astype(jnp.float32).reshape(rows, corner_width)
    if first_out.shape[-1] > edge_width:
        first_out[:, :, corner_part] = second_in[:, :, corner_part]

    tile = edge_width // 3 if edge_width % 3 == 0 else edge_width
    steps = edge_width // tile
    for step in range(steps):
        at = pl.ds(step * tile, tile)
        value = jnp.dot(left[...], operators[direction, :, at], preferred_element_type=jnp.float32)
        source = sources[direction, tick % 2, :, :, at].astype(jnp.float32).reshape(rows, tile)
        first = value[:rows] + source
        second = value[rows:] + source
        for end in range(2):
            if step != (steps - 1 if end else 0):
                continue
            here = slice(tile - corner_width, tile) if end else slice(0, corner_width)
            added = jnp.where(direction == end, corner, 0.0)
            widths = ((0, 0), (tile - corner_width, 0) if end else (0, tile - corner_width))
            added = jnp.pad(added, widths)
            first = first + added
            second = second + added
            given = (0.5 * (first[:, here] + second[:, here])).astype(second_out.dtype)
            given = given.reshape(parts, shots, corner_width)

            @pl.when(direction != end)
            def _():
                second_out[:, :, corner_part] = given

        first_out[:, :, at] = first.astype(first_out.dtype).reshape(parts, shots, tile)
        second_out[:, :, at] = second.astype(second_out.dtype).reshape(parts, shots, tile)
        act(step, at)


def middle_kernel(
    tick, stream, corner_width, first_in, second_in, corner_in, sources, operators, *refs
):
    outs, left = refs[:-1], refs[-1]
    compute(
        tick, stream, corner_width, first_in, second_in, corner_in, sources, operators, outs, left,
        lambda step, at: None,
    )


def last_kernel(
    tick, stream, histories, corner_width, flags, first_in, second_in, sources, operators, *refs
):
    count = len(histories)
    older = [refs[2 * i : 2 * i + 2] for i in range(count)]
    refs = refs[2 * count :]
    if not count:
        refs = refs[4:]
    edges_out, corners_out, (left, *outs, old_sems, sems) = refs[0:2], refs[2:4], refs[4:]
    edge_width = sources.shape[-1]
    edge_part = pl.ds(0, edge_width)
    corner_part = pl.ds(edge_width, corner_width)

    batches = {}
    for at_tick in (tick - 1, tick) if count else (tick,):
        chosen = jnp.max(flags[own_direction(at_tick, stream), :1]).astype(jnp.int32)
        batches[at_tick, stream] = 1 - chosen if at_tick % 2 else chosen
    if count:
        chosen = jnp.max(flags[own_direction(tick - 1, 1 - stream), :1]).astype(jnp.int32)
        batches[tick - 1, 1 - stream] = 1 - chosen if (tick - 1) % 2 else chosen

    def each(at_tick, at_stream, act_on):
        for direction in range(2):

            @pl.when(own_direction(at_tick, at_stream) == direction)
            def _():
                batch = batches[at_tick, at_stream]
                act_on(edges_out[direction], corners_out[direction], batch)

    def old_stores(index, act):
        first, second = older[index]

        def act_on(edges, corners, batch):
            pairs = (
                (first.at[:, :, edge_part], edges.at[0, batch]),
                (second.at[:, :, edge_part], edges.at[1, batch]),
                (second.at[:, :, corner_part], corners.at[batch]),
            )
            for place, (source, target) in enumerate(pairs):
                act(pltpu.make_async_copy(source, target, old_sems.at[index, place]))

        each(tick - 1, histories[index], act_on)

    def tile_store(act, step, at):
        def act_on(edges, corners, batch):
            for slot in range(2):
                act(
                    pltpu.make_async_copy(
                        outs[slot].at[:, :, at], edges.at[slot, batch, :, :, at],
                        sems.at[slot, step],
                    )
                )

        each(tick, stream, act_on)

    def corner_store(act):
        each(
            tick, stream,
            lambda edges, corners, batch: act(
                pltpu.make_async_copy(
                    outs[1].at[:, :, corner_part], corners.at[batch], sems.at[2, 0]
                )
            ),
        )

    for index in range(count):
        old_stores(index, start)
    tiles = []

    def stored(step, at):
        tiles.append((step, at))
        tile_store(start, step, at)

    compute(
        tick, stream, corner_width, first_in, second_in, None, sources, operators, outs, left,
        stored,
    )
    corner_store(start)
    for index in range(count):
        old_stores(index, wait)
    for step, at in tiles:
        tile_store(wait, step, at)
    corner_store(wait)


def tick_shapes(sources, corner_width, tick, ticks):
    _, _, parts, shots, edge_width = sources.shape
    kind = sources.dtype
    first_width = edge_width + (0 if tick == ticks - 1 else corner_width)
    return [
        pltpu.VMEM((parts, shots, first_width), kind),
        pltpu.VMEM((parts, shots, edge_width + corner_width), kind),
    ]


def cost(heavy):
    return pl.CostEstimate(flops=10**10 if heavy else 0, bytes_accessed=1, transcendentals=0)


def left_side(sources):
    _, _, parts, shots, edge_width = sources.shape
    return pltpu.VMEM((2 * parts * shots, 4 * edge_width), sources.dtype)


def middle_tick(tick, ticks, stream, first_in, second_in, corner_in, sources, operators):
    shapes = tick_shapes(sources, corner_in.shape[-1], tick, ticks)
    return pl.pallas_call(
        functools.partial(middle_kernel, tick, stream, corner_in.shape[-1]),
        out_shape=shapes,
        in_specs=[VMEM] * 5,
        out_specs=[VMEM] * len(shapes),
        scratch_shapes=[left_side(sources)],
        compiler_params=pltpu.CompilerParams(vmem_limit_bytes=VMEM_LIMIT),
        cost_estimate=cost(tick == 0 and stream == 0),
        name="tick" + str(tick) + "_stream" + str(stream),
    )(first_in, second_in, corner_in, sources, operators)


def last_tick(
    tick, ticks, stream, flags, first_in, second_in, sources, operators, history, so_far,
    corner_width,
):
    _, batches, parts, shots, edge_width = sources.shape
    kind = sources.dtype
    outs = [jax.ShapeDtypeStruct((2, batches, parts, shots, edge_width), kind)] * 2
    outs += [jax.ShapeDtypeStruct((batches, parts, shots, corner_width), kind)] * 2
    operands = [flags, first_in, second_in, sources, operators]
    in_specs = [VMEM] * 5
    aliases = {}
    if so_far is None:
        for traces in history:
            operands += list(traces)
        in_specs += [VMEM] * 4
        histories = (0, 1)
    else:
        aliases = {len(operands) + i: i for i in range(4)}
        operands += list(so_far)
        in_specs += [HBM] * 4
        histories = ()
    return pl.pallas_call(
        functools.partial(last_kernel, tick, stream, histories, corner_width),
        out_shape=outs,
        in_specs=in_specs,
        out_specs=[HBM] * 4,
        scratch_shapes=[left_side(sources)]
        + tick_shapes(sources, corner_width, tick, ticks)
        + [pltpu.SemaphoreType.DMA((2, 3)), pltpu.SemaphoreType.DMA((3, 3))],
        input_output_aliases=aliases,
        compiler_params=pltpu.CompilerParams(vmem_limit_bytes=VMEM_LIMIT),
        cost_estimate=cost(False),
        name="tick" + str(tick) + "_stream" + str(stream),
    )(*operands)


def move(array, counts, step_of_cell):
    row_count, col_count = counts
    pairs = []
    for row in range(row_count):
        for col in range(col_count):
            down, right = step_of_cell(row, col)
            to_row = (row + down) % row_count
            to_col = (col + right) % col_count
            pairs.append((row * col_count + col, to_row * col_count + to_col))
    return lax.ppermute(array, ("row", "col"), pairs)


def sense(row, col, tick, stream):
    return -1 if direction_at(row, col, tick, stream) else 1


def by_row(array, counts, tick, stream):
    return move(array, counts, lambda row, col: (sense(row, col, tick - 1, stream), 0))


def by_col(array, counts, tick, stream):
    return move(array, counts, lambda row, col: (0, sense(row, col, tick - 1, stream)))


def by_diagonal(array, counts, stream):
    return move(array, counts, lambda row, col: (sense(row, col, 0, stream),) * 2)


def shards(
    southeast_edges, northwest_edges, southeast_corners, northwest_corners, operators, sources,
    roster,
):
    counts = (lax.axis_size("row"), lax.axis_size("col"))
    ticks = roster.shape[1]
    corner_width = southeast_corners.shape[-1]
    roster = in_hbm(roster.transpose(0, 2, 1))
    states = (
        southeast_edges[0, 0], northwest_edges[0, 0], southeast_corners[0, 0],
        northwest_corners[0, 0],
    )
    slots = [select_initial(counts, 0, roster, states), None]
    *rest, prepared, picked, flags = load_operators(
        counts, 1, roster, states, operators[0, 0], sources[0, 0]
    )
    slots[1] = rest
    corners = [None, None]
    firsts = [slots[stream][0] for stream in range(2)]
    seconds = [slots[stream][1] for stream in range(2)]
    outs = None
    for tick in range(ticks):
        done = []
        for stream in range(2):
            second_in = by_col(seconds[stream], counts, tick, stream)
            if tick == 0:
                corners[stream] = by_diagonal(slots[stream][2], counts, stream)
            first_in = by_row(firsts[stream], counts, tick, stream)
            if tick < ticks - 1:
                done.append(
                    middle_tick(
                        tick, ticks, stream, first_in, second_in, corners[stream], picked, prepared
                    )
                )
            else:
                outs = last_tick(
                    tick, ticks, stream, flags, first_in, second_in, picked, prepared, history, outs,
                    corner_width,
                )
        if tick < ticks - 1:
            history = done
            firsts = [done[0][0], done[1][0]]
            seconds = [done[0][1], done[1][1]]
    return tuple(array[None, None] for array in outs)


def solution(mesh):
    edges = P("row", "col", None, None, None, None, None)
    corners = P("row", "col", None, None, None, None)
    return jax.shard_map(
        shards,
        mesh=mesh,
        in_specs=(edges, edges, corners, corners, corners, corners, P()),
        out_specs=(edges, edges, corners, corners),
        check_vma=False,
    )
```

```python
import functools

import jax
import jax.numpy as jnp
from jax import lax
from jax.experimental import pallas as pl
from jax.experimental.pallas import tpu as pltpu
from jax.sharding import PartitionSpec as P

VMEM = pl.BlockSpec(memory_space=pltpu.VMEM)
SMEM = pl.BlockSpec(memory_space=pltpu.SMEM)
HBM = pl.BlockSpec(memory_space=pltpu.HBM)
VMEM_LIMIT = 40 * 1024 * 1024
FIRST = 10**10
MIDDLE = 8 * 10**8


def direction_at(row, col, tick, stream):
    return (row + col + tick + 1 + stream) % 2


def in_hbm(array):
    return pltpu.with_memory_space_constraint(array, pltpu.HBM)


def own_direction(tick, stream):
    return direction_at(lax.axis_index("row"), lax.axis_index("col"), tick, stream)


def chosen_at_start(roster_ref, direction, counts):
    row = lax.axis_index("row")
    col = lax.axis_index("col")
    if direction:
        row = counts[0] - 1 - row
        col = counts[1] - 1 - col
    klass = lax.rem(row + col, 2)
    return jnp.where(roster_ref[direction, 0, 0] == klass, 0, 1)


def start(copy):
    copy.start()


def wait(copy):
    copy.wait()


def select_slots(counts, stream, roster, edges, corners, outs, sems, act):
    by_row, by_col, by_diagonal = outs
    edge_width = by_row.shape[-1]
    corner_width = by_diagonal.shape[-1]
    for going in range(2):

        @pl.when(own_direction(-1, stream) == going)
        def _():
            other = 1 - chosen_at_start(roster, going, counts)
            own = going if False else 1 - going
            mine = chosen_at_start(roster, own, counts)
            pairs = (
                (edges[going].at[0, other], by_row),
                (corners[own].at[mine], by_diagonal.at[0]),
                (corners[own].at[1 - mine], by_diagonal.at[1]),
                (edges[going].at[1, other], by_col.at[:, :, pl.ds(0, edge_width)]),
                (corners[going].at[other], by_col.at[:, :, pl.ds(edge_width, corner_width)]),
            )
            for index, (source, target) in enumerate(pairs):
                act(pltpu.make_async_copy(source, target, sems.at[index]))


def select_kernel(
    counts, stream, roster, se_edges, nw_edges, se_corners, nw_corners, by_row, by_col, by_diagonal,
    numbers, all_edges, all_corners, sems
):
    edges, corners = (se_edges, nw_edges), (se_corners, nw_corners)
    roster_copy = pltpu.make_async_copy(roster, numbers, sems.at[0])
    roster_copy.start()
    own = 1 - own_direction(-1, stream)

    def fetch(act):
        for going in range(2):

            @pl.when(own_direction(-1, stream) == going)
            def _():
                act(pltpu.make_async_copy(edges[going], all_edges, sems.at[1]))
                act(pltpu.make_async_copy(corners[1 - going], all_corners, sems.at[2]))

    fetch(start)
    roster_copy.wait()
    chosen = [chosen_at_start(numbers, direction, counts) for direction in range(2)]
    other = 1 - jnp.where(own == 0, chosen[1], chosen[0])
    mine = jnp.where(own == 0, chosen[0], chosen[1])
    fetch(wait)
    by_row[...] = all_edges[0, other]
    by_col[...] = all_edges[1, other]
    by_diagonal[...] = all_corners[mine]


def slot_shapes(edges, corners, late):
    _, _, parts, shots, edge_width = edges.shape
    corner_width = corners.shape[-1]
    kind = edges.dtype
    return [
        pltpu.VMEM((parts, shots, edge_width), kind),
        pltpu.VMEM((parts, shots, edge_width + (corner_width if late else 0)), kind),
        pltpu.VMEM(((2,) if late else ()) + (parts, shots, corner_width), kind),
    ]


def select_initial(counts, stream, roster, states):
    edges, _, corners, _ = states
    return pl.pallas_call(
        functools.partial(select_kernel, counts, stream),
        out_shape=slot_shapes(edges, corners, False),
        in_specs=[HBM] * 5,
        out_specs=[VMEM] * 3,
        scratch_shapes=[
            pltpu.SMEM(roster.shape, roster.dtype),
            pltpu.VMEM(edges.shape, edges.dtype),
            pltpu.VMEM(corners.shape, corners.dtype),
            pltpu.SemaphoreType.DMA((3,)),
        ],
        compiler_params=pltpu.CompilerParams(vmem_limit_bytes=VMEM_LIMIT),
        name="select_initial",
    )(roster, *map(in_hbm, states))


def load_kernel(
    counts, stream, roster, se_edges, nw_edges, se_corners, nw_corners, operators, sources, *refs
):
    outs = refs[:3]
    prepared, picked, flags, select_sems, operator_sems, source_sems = refs[3:]
    count, edge_width, _ = operators.shape
    copies = [
        pltpu.make_async_copy(
            operators.at[i],
            prepared.at[0, pl.ds(i * edge_width, edge_width)],
            operator_sems.at[i],
        )
        for i in range(count)
    ]
    source_copies = []
    for direction in range(2):
        mine = chosen_at_start(roster, direction, counts)
        flags[direction] = jnp.full(flags.shape[1:], mine.astype(jnp.float32))
        for late in range(2):
            source_copies.append(
                pltpu.make_async_copy(
                    sources.at[1 - mine if late else mine],
                    picked.at[direction, late],
                    source_sems.at[direction, late],
                )
            )
    edges, corners = (se_edges, nw_edges), (se_corners, nw_corners)
    for copy in copies:
        copy.start()
    select_slots(counts, stream, roster, edges, corners, outs, select_sems, start)
    for copy in source_copies:
        copy.start()
    for i in range(count):
        copies[i].wait()
        rows = pl.ds(i * edge_width, edge_width)
        prepared[1, rows, :] = prepared[0, rows, :].T
    select_slots(counts, stream, roster, edges, corners, outs, select_sems, wait)
    for copy in source_copies:
        copy.wait()


def load_operators(counts, stream, roster, states, operators, sources):
    count = operators.shape[0] * operators.shape[1]
    edge_width = operators.shape[-1]
    kind = operators.dtype
    operators = operators.reshape(count, edge_width, edge_width)
    return pl.pallas_call(
        functools.partial(load_kernel, counts, stream),
        out_shape=slot_shapes(states[0], states[2], True)
        + [
            pltpu.VMEM((2, count * edge_width, edge_width), kind),
            pltpu.VMEM((2,) + sources.shape, kind),
            pltpu.VMEM((2, 8, 128), jnp.float32),
        ],
        in_specs=[SMEM] + [HBM] * 6,
        out_specs=[VMEM] * 6,
        scratch_shapes=[
            pltpu.SemaphoreType.DMA((5,)),
            pltpu.SemaphoreType.DMA((count,)),
            pltpu.SemaphoreType.DMA((2, 2)),
        ],
        compiler_params=pltpu.CompilerParams(vmem_limit_bytes=VMEM_LIMIT),
        cost_estimate=cost(0),
        name="load_operators",
    )(roster, *map(in_hbm, states), in_hbm(operators), in_hbm(sources))


def compute(
    tick, stream, corner_width, first_in, second_in, corner_in, sources, operators, outs, left, act
):
    first_out, second_out = outs
    parts, shots, edge_width = sources.shape[2:]
    rows = parts * shots
    direction = own_direction(tick, stream)
    edge_part = pl.ds(0, edge_width)
    corner_part = pl.ds(edge_width, corner_width)

    for place, ref in ((0, first_in), (2, second_in)):
        other_place = 2 - place
        real = ref[0, :, edge_part]
        imag = ref[1, :, edge_part]
        minus = -imag
        for slot, block in ((place, 0), (other_place, 1)):
            row = block * rows
            column = slot * edge_width
            left[pl.ds(row, shots), pl.ds(column, edge_width)] = real
            left[pl.ds(row + shots, shots), pl.ds(column, edge_width)] = imag
            left[pl.ds(row, shots), pl.ds(column + edge_width, edge_width)] = minus
            left[pl.ds(row + shots, shots), pl.ds(column + edge_width, edge_width)] = real

    if corner_in is None:
        corner = first_in[:, :, corner_part]
    else:
        corner = corner_in[...] if len(corner_in.shape) == 3 else corner_in[tick]
    corner = corner.astype(jnp.float32).reshape(rows, corner_width)
    if first_out.shape[-1] > edge_width:
        first_out[:, :, corner_part] = second_in[:, :, corner_part]

    tile = edge_width // 3 if edge_width % 3 == 0 else edge_width
    steps = edge_width // tile
    for step in range(steps):
        at = pl.ds(step * tile, tile)
        value = jnp.dot(left[...], operators[direction, :, at], preferred_element_type=jnp.float32)
        source = sources[direction, tick % 2, :, :, at].astype(jnp.float32).reshape(rows, tile)
        first = value[:rows] + source
        second = value[rows:] + source
        for end in range(2):
            if step != (steps - 1 if end else 0):
                continue
            here = slice(tile - corner_width, tile) if end else slice(0, corner_width)
            added = jnp.where(direction == end, corner, 0.0)
            widths = ((0, 0), (tile - corner_width, 0) if end else (0, tile - corner_width))
            added = jnp.pad(added, widths)
            first = first + added
            second = second + added
            given = (0.5 * (first[:, here] + second[:, here])).astype(second_out.dtype)
            given = given.reshape(parts, shots, corner_width)

            @pl.when(direction != end)
            def _():
                second_out[:, :, corner_part] = given

        first_out[:, :, at] = first.astype(first_out.dtype).reshape(parts, shots, tile)
        second_out[:, :, at] = second.astype(second_out.dtype).reshape(parts, shots, tile)
        act(step, at)


def middle_kernel(
    tick, stream, corner_width, first_in, second_in, sources, operators, *refs
):
    *corner_in, first_out, second_out, left = refs
    outs = (first_out, second_out)
    corner_in = corner_in[0] if corner_in else None
    compute(
        tick, stream, corner_width, first_in, second_in, corner_in, sources, operators, outs, left,
        lambda step, at: None,
    )


def last_kernel(
    tick, stream, histories, corner_width, flags, first_in, second_in, sources, operators, *refs
):
    count = len(histories)
    older = [refs[2 * i : 2 * i + 2] for i in range(count)]
    refs = refs[2 * count :]
    if not count:
        refs = refs[4:]
    edges_out, corners_out, (left, *outs, old_sems, sems) = refs[0:2], refs[2:4], refs[4:]
    edge_width = sources.shape[-1]
    edge_part = pl.ds(0, edge_width)
    corner_part = pl.ds(edge_width, corner_width)

    batches = {}
    for at_tick in (tick - 1, tick) if count else (tick,):
        chosen = jnp.max(flags[own_direction(at_tick, stream), :1]).astype(jnp.int32)
        batches[at_tick, stream] = 1 - chosen if at_tick % 2 else chosen
    if count:
        chosen = jnp.max(flags[own_direction(tick - 1, 1 - stream), :1]).astype(jnp.int32)
        batches[tick - 1, 1 - stream] = 1 - chosen if (tick - 1) % 2 else chosen

    def each(at_tick, at_stream, act_on):
        for direction in range(2):

            @pl.when(own_direction(at_tick, at_stream) == direction)
            def _():
                batch = batches[at_tick, at_stream]
                act_on(edges_out[direction], corners_out[direction], batch)

    def old_stores(index, act):
        first, second = older[index]

        def act_on(edges, corners, batch):
            pairs = (
                (first.at[:, :, edge_part], edges.at[0, batch]),
                (second.at[:, :, edge_part], edges.at[1, batch]),
                (second.at[:, :, corner_part], corners.at[batch]),
            )
            for place, (source, target) in enumerate(pairs):
                act(pltpu.make_async_copy(source, target, old_sems.at[index, place]))

        each(tick - 1, histories[index], act_on)

    def tile_store(act, step, at):
        def act_on(edges, corners, batch):
            for slot in range(2):
                act(
                    pltpu.make_async_copy(
                        outs[slot].at[:, :, at], edges.at[slot, batch, :, :, at],
                        sems.at[slot, step],
                    )
                )

        each(tick, stream, act_on)

    def corner_store(act):
        each(
            tick, stream,
            lambda edges, corners, batch: act(
                pltpu.make_async_copy(
                    outs[1].at[:, :, corner_part], corners.at[batch], sems.at[2, 0]
                )
            ),
        )

    for index in range(count):
        old_stores(index, start)
    tiles = []

    def stored(step, at):
        tiles.append((step, at))
        tile_store(start, step, at)

    compute(
        tick, stream, corner_width, first_in, second_in, None, sources, operators, outs, left,
        stored,
    )
    corner_store(start)
    for index in range(count):
        old_stores(index, wait)
    for step, at in tiles:
        tile_store(wait, step, at)
    corner_store(wait)


def tick_shapes(sources, corner_width, tick, ticks, stream):
    _, _, parts, shots, edge_width = sources.shape
    kind = sources.dtype
    first_width = edge_width + (0 if tick == ticks - 1 or tick + stream == 0 else corner_width)
    return [
        pltpu.VMEM((parts, shots, first_width), kind),
        pltpu.VMEM((parts, shots, edge_width + corner_width), kind),
    ]


def cost(flops):
    return pl.CostEstimate(flops=flops, bytes_accessed=1, transcendentals=0)


def left_side(sources):
    _, _, parts, shots, edge_width = sources.shape
    return pltpu.VMEM((2 * parts * shots, 4 * edge_width), sources.dtype)


def middle_tick(
    tick, ticks, stream, first_in, second_in, sources, operators, corner_width, corner_in
):
    shapes = tick_shapes(sources, corner_width, tick, ticks, stream)
    operands = [first_in, second_in, sources, operators]
    if corner_in is not None:
        operands.append(corner_in)
    return pl.pallas_call(
        functools.partial(middle_kernel, tick, stream, corner_width),
        out_shape=shapes,
        in_specs=[VMEM] * len(operands),
        out_specs=[VMEM] * len(shapes),
        scratch_shapes=[left_side(sources)],
        compiler_params=pltpu.CompilerParams(vmem_limit_bytes=VMEM_LIMIT),
        cost_estimate=cost(0 if stream else FIRST if tick == 0 else MIDDLE),
        name="tick" + str(tick) + "_stream" + str(stream),
    )(*operands)


def last_tick(
    tick, ticks, stream, flags, first_in, second_in, sources, operators, history, so_far,
    corner_width,
):
    _, batches, parts, shots, edge_width = sources.shape
    kind = sources.dtype
    outs = [jax.ShapeDtypeStruct((2, batches, parts, shots, edge_width), kind)] * 2
    outs += [jax.ShapeDtypeStruct((batches, parts, shots, corner_width), kind)] * 2
    operands = [flags, first_in, second_in, sources, operators]
    in_specs = [VMEM] * 5
    aliases = {}
    if so_far is None:
        for traces in history:
            operands += list(traces)
        in_specs += [VMEM] * 4
        histories = (0, 1)
    else:
        aliases = {len(operands) + i: i for i in range(4)}
        operands += list(so_far)
        in_specs += [HBM] * 4
        histories = ()
    return pl.pallas_call(
        functools.partial(last_kernel, tick, stream, histories, corner_width),
        out_shape=outs,
        in_specs=in_specs,
        out_specs=[HBM] * 4,
        scratch_shapes=[left_side(sources)]
        + tick_shapes(sources, corner_width, tick, ticks, stream)
        + [pltpu.SemaphoreType.DMA((2, 3)), pltpu.SemaphoreType.DMA((3, 3))],
        input_output_aliases=aliases,
        compiler_params=pltpu.CompilerParams(vmem_limit_bytes=VMEM_LIMIT),
        cost_estimate=cost(0),
        name="tick" + str(tick) + "_stream" + str(stream),
    )(*operands)


def move(array, counts, step_of_cell):
    row_count, col_count = counts
    pairs = []
    for row in range(row_count):
        for col in range(col_count):
            down, right = step_of_cell(row, col)
            to_row = (row + down) % row_count
            to_col = (col + right) % col_count
            pairs.append((row * col_count + col, to_row * col_count + to_col))
    return lax.ppermute(array, ("row", "col"), pairs)


def sense(row, col, tick, stream):
    return -1 if direction_at(row, col, tick, stream) else 1


def by_row(array, counts, tick, stream):
    return move(array, counts, lambda row, col: (sense(row, col, tick - 1, stream), 0))


def by_col(array, counts, tick, stream):
    return move(array, counts, lambda row, col: (0, sense(row, col, tick - 1, stream)))


def by_diagonal(array, counts, stream):
    return move(array, counts, lambda row, col: (sense(row, col, 0, stream),) * 2)


def shards(
    southeast_edges, northwest_edges, southeast_corners, northwest_corners, operators, sources,
    roster,
):
    counts = (lax.axis_size("row"), lax.axis_size("col"))
    ticks = roster.shape[1]
    corner_width = southeast_corners.shape[-1]
    roster = in_hbm(roster.transpose(0, 2, 1))
    states = (
        southeast_edges[0, 0], northwest_edges[0, 0], southeast_corners[0, 0],
        northwest_corners[0, 0],
    )
    slots = [select_initial(counts, 0, roster, states), None]
    *rest, prepared, picked, flags = load_operators(
        counts, 1, roster, states, operators[0, 0], sources[0, 0]
    )
    slots[1] = rest
    corners = [None, None]
    firsts = [slots[stream][0] for stream in range(2)]
    seconds = [slots[stream][1] for stream in range(2)]
    outs = None
    for tick in range(ticks):
        done = []
        for stream in range(2):
            second_in = by_col(seconds[stream], counts, tick, stream)
            if tick == 0:
                corners[stream] = by_diagonal(slots[stream][2], counts, stream)
            first_in = by_row(firsts[stream], counts, tick, stream)
            if tick < ticks - 1:
                corner_in = corners[stream] if tick == 0 else None
                if tick == 1 and stream == 0:
                    corner_in = corners[1]
                done.append(
                    middle_tick(
                        tick, ticks, stream, first_in, second_in, picked, prepared, corner_width,
                        corner_in,
                    )
                )
            else:
                outs = last_tick(
                    tick, ticks, stream, flags, first_in, second_in, picked, prepared, history, outs,
                    corner_width,
                )
        if tick < ticks - 1:
            history = done
            firsts = [done[0][0], done[1][0]]
            seconds = [done[0][1], done[1][1]]
    return tuple(array[None, None] for array in outs)


def solution(mesh):
    edges = P("row", "col", None, None, None, None, None)
    corners = P("row", "col", None, None, None, None)
    return jax.shard_map(
        shards,
        mesh=mesh,
        in_specs=(edges, edges, corners, corners, corners, corners, P()),
        out_specs=(edges, edges, corners, corners),
        check_vma=False,
    )
```

```python
import functools

import jax
import jax.numpy as jnp
from jax import lax
from jax.experimental import pallas as pl
from jax.experimental.pallas import tpu as pltpu
from jax.sharding import PartitionSpec as P

VMEM = pl.BlockSpec(memory_space=pltpu.VMEM)
SMEM = pl.BlockSpec(memory_space=pltpu.SMEM)
HBM = pl.BlockSpec(memory_space=pltpu.HBM)
VMEM_LIMIT = 40 * 1024 * 1024
FIRST = 2000 * 10**6
MIDDLE = 8 * 10**8


def direction_at(row, col, tick, stream):
    return (row + col + tick + 1 + stream) % 2


def in_hbm(array):
    return pltpu.with_memory_space_constraint(array, pltpu.HBM)


def own_direction(tick, stream):
    return direction_at(lax.axis_index("row"), lax.axis_index("col"), tick, stream)


def chosen_at_start(roster_ref, direction, counts):
    row = lax.axis_index("row")
    col = lax.axis_index("col")
    if direction:
        row = counts[0] - 1 - row
        col = counts[1] - 1 - col
    klass = lax.rem(row + col, 2)
    return jnp.where(roster_ref[direction, 0, 0] == klass, 0, 1)


def start(copy):
    copy.start()


def wait(copy):
    copy.wait()


def select_slots(counts, stream, roster, edges, corners, outs, sems, act):
    by_row, by_col, by_diagonal = outs
    edge_width = by_row.shape[-1]
    corner_width = by_diagonal.shape[-1]
    for going in range(2):

        @pl.when(own_direction(-1, stream) == going)
        def _():
            other = 1 - chosen_at_start(roster, going, counts)
            own = going if False else 1 - going
            mine = chosen_at_start(roster, own, counts)
            pairs = (
                (edges[going].at[0, other], by_row),
                (corners[own].at[mine], by_diagonal.at[0]),
                (corners[own].at[1 - mine], by_diagonal.at[1]),
                (edges[going].at[1, other], by_col.at[:, :, pl.ds(0, edge_width)]),
                (corners[going].at[other], by_col.at[:, :, pl.ds(edge_width, corner_width)]),
            )
            for index, (source, target) in enumerate(pairs):
                act(pltpu.make_async_copy(source, target, sems.at[index]))


def select_kernel(
    counts, stream, roster, se_edges, nw_edges, se_corners, nw_corners, by_row, by_col, by_diagonal,
    numbers, all_edges, all_corners, sems
):
    edges, corners = (se_edges, nw_edges), (se_corners, nw_corners)
    roster_copy = pltpu.make_async_copy(roster, numbers, sems.at[0])
    roster_copy.start()
    own = 1 - own_direction(-1, stream)

    def fetch(act):
        for going in range(2):

            @pl.when(own_direction(-1, stream) == going)
            def _():
                act(pltpu.make_async_copy(edges[going], all_edges, sems.at[1]))
                act(pltpu.make_async_copy(corners[1 - going], all_corners, sems.at[2]))

    fetch(start)
    roster_copy.wait()
    chosen = [chosen_at_start(numbers, direction, counts) for direction in range(2)]
    other = 1 - jnp.where(own == 0, chosen[1], chosen[0])
    mine = jnp.where(own == 0, chosen[0], chosen[1])
    fetch(wait)
    by_row[...] = all_edges[0, other]
    by_col[...] = all_edges[1, other]
    by_diagonal[...] = all_corners[mine]


def slot_shapes(edges, corners, late):
    _, _, parts, shots, edge_width = edges.shape
    corner_width = corners.shape[-1]
    kind = edges.dtype
    return [
        pltpu.VMEM((parts, shots, edge_width), kind),
        pltpu.VMEM((parts, shots, edge_width + (corner_width if late else 0)), kind),
        pltpu.VMEM(((2,) if late else ()) + (parts, shots, corner_width), kind),
    ]


def select_initial(counts, stream, roster, states):
    edges, _, corners, _ = states
    return pl.pallas_call(
        functools.partial(select_kernel, counts, stream),
        out_shape=slot_shapes(edges, corners, False),
        in_specs=[HBM] * 5,
        out_specs=[VMEM] * 3,
        scratch_shapes=[
            pltpu.SMEM(roster.shape, roster.dtype),
            pltpu.VMEM(edges.shape, edges.dtype),
            pltpu.VMEM(corners.shape, corners.dtype),
            pltpu.SemaphoreType.DMA((3,)),
        ],
        compiler_params=pltpu.CompilerParams(vmem_limit_bytes=VMEM_LIMIT),
        name="select_initial",
    )(roster, *map(in_hbm, states))


def load_kernel(
    counts, stream, roster, se_edges, nw_edges, se_corners, nw_corners, operators, sources, *refs
):
    outs = refs[:3]
    prepared, picked, flags, select_sems, operator_sems, source_sems = refs[3:]
    count, edge_width, _ = operators.shape
    copies = [
        pltpu.make_async_copy(
            operators.at[i],
            prepared.at[0, pl.ds(i * edge_width, edge_width)],
            operator_sems.at[i],
        )
        for i in range(count)
    ]
    source_copies = []
    for direction in range(2):
        mine = chosen_at_start(roster, direction, counts)
        flags[direction] = jnp.full(flags.shape[1:], mine.astype(jnp.float32))
        for late in range(2):
            source_copies.append(
                pltpu.make_async_copy(
                    sources.at[1 - mine if late else mine],
                    picked.at[direction, late],
                    source_sems.at[direction, late],
                )
            )
    edges, corners = (se_edges, nw_edges), (se_corners, nw_corners)
    for copy in copies:
        copy.start()
    select_slots(counts, stream, roster, edges, corners, outs, select_sems, start)
    for copy in source_copies:
        copy.start()
    for i in range(count):
        copies[i].wait()
        rows = pl.ds(i * edge_width, edge_width)
        prepared[1, rows, :] = prepared[0, rows, :].T
    select_slots(counts, stream, roster, edges, corners, outs, select_sems, wait)
    for copy in source_copies:
        copy.wait()


def load_operators(counts, stream, roster, states, operators, sources):
    count = operators.shape[0] * operators.shape[1]
    edge_width = operators.shape[-1]
    kind = operators.dtype
    operators = operators.reshape(count, edge_width, edge_width)
    return pl.pallas_call(
        functools.partial(load_kernel, counts, stream),
        out_shape=slot_shapes(states[0], states[2], True)
        + [
            pltpu.VMEM((2, count * edge_width, edge_width), kind),
            pltpu.VMEM((2,) + sources.shape, kind),
            pltpu.VMEM((2, 8, 128), jnp.float32),
        ],
        in_specs=[SMEM] + [HBM] * 6,
        out_specs=[VMEM] * 6,
        scratch_shapes=[
            pltpu.SemaphoreType.DMA((5,)),
            pltpu.SemaphoreType.DMA((count,)),
            pltpu.SemaphoreType.DMA((2, 2)),
        ],
        compiler_params=pltpu.CompilerParams(vmem_limit_bytes=VMEM_LIMIT),
        cost_estimate=cost(0),
        name="load_operators",
    )(roster, *map(in_hbm, states), in_hbm(operators), in_hbm(sources))


def compute(
    tick, stream, corner_width, first_in, second_in, corner_in, sources, operators, outs, left, act
):
    first_out, second_out = outs
    parts, shots, edge_width = sources.shape[2:]
    rows = parts * shots
    direction = own_direction(tick, stream)
    edge_part = pl.ds(0, edge_width)
    corner_part = pl.ds(edge_width, corner_width)

    for place, ref in ((0, first_in), (2, second_in)):
        other_place = 2 - place
        real = ref[0, :, edge_part]
        imag = ref[1, :, edge_part]
        minus = -imag
        for slot, block in ((place, 0), (other_place, 1)):
            row = block * rows
            column = slot * edge_width
            left[pl.ds(row, shots), pl.ds(column, edge_width)] = real
            left[pl.ds(row + shots, shots), pl.ds(column, edge_width)] = imag
            left[pl.ds(row, shots), pl.ds(column + edge_width, edge_width)] = minus
            left[pl.ds(row + shots, shots), pl.ds(column + edge_width, edge_width)] = real

    if corner_in is None:
        corner = first_in[:, :, corner_part]
    else:
        corner = corner_in[...] if len(corner_in.shape) == 3 else corner_in[tick]
    corner = corner.astype(jnp.float32).reshape(rows, corner_width)
    if first_out.shape[-1] > edge_width:
        first_out[:, :, corner_part] = second_in[:, :, corner_part]

    tile = edge_width // 3 if edge_width % 3 == 0 else edge_width
    steps = edge_width // tile
    for step in range(steps):
        at = pl.ds(step * tile, tile)
        value = jnp.dot(left[...], operators[direction, :, at], preferred_element_type=jnp.float32)
        source = sources[direction, tick % 2, :, :, at].astype(jnp.float32).reshape(rows, tile)
        first = value[:rows] + source
        second = value[rows:] + source
        for end in range(2):
            if step != (steps - 1 if end else 0):
                continue
            here = slice(tile - corner_width, tile) if end else slice(0, corner_width)
            added = jnp.where(direction == end, corner, 0.0)
            widths = ((0, 0), (tile - corner_width, 0) if end else (0, tile - corner_width))
            added = jnp.pad(added, widths)
            first = first + added
            second = second + added
            given = (0.5 * (first[:, here] + second[:, here])).astype(second_out.dtype)
            given = given.reshape(parts, shots, corner_width)

            @pl.when(direction != end)
            def _():
                second_out[:, :, corner_part] = given

        first_out[:, :, at] = first.astype(first_out.dtype).reshape(parts, shots, tile)
        second_out[:, :, at] = second.astype(second_out.dtype).reshape(parts, shots, tile)
        act(step, at)


def middle_kernel(
    tick, stream, corner_width, first_in, second_in, sources, operators, *refs
):
    *corner_in, first_out, second_out, left = refs
    outs = (first_out, second_out)
    corner_in = corner_in[0] if corner_in else None
    compute(
        tick, stream, corner_width, first_in, second_in, corner_in, sources, operators, outs, left,
        lambda step, at: None,
    )


def last_kernel(
    tick, stream, histories, corner_width, flags, first_in, second_in, sources, operators, *refs
):
    count = len(histories)
    older = [refs[2 * i : 2 * i + 2] for i in range(count)]
    refs = refs[2 * count :]
    if not count:
        refs = refs[4:]
    edges_out, corners_out, (left, *outs, old_sems, sems) = refs[0:2], refs[2:4], refs[4:]
    edge_width = sources.shape[-1]
    edge_part = pl.ds(0, edge_width)
    corner_part = pl.ds(edge_width, corner_width)

    batches = {}
    for at_tick in (tick - 1, tick) if count else (tick,):
        chosen = jnp.max(flags[own_direction(at_tick, stream), :1]).astype(jnp.int32)
        batches[at_tick, stream] = 1 - chosen if at_tick % 2 else chosen
    if count:
        chosen = jnp.max(flags[own_direction(tick - 1, 1 - stream), :1]).astype(jnp.int32)
        batches[tick - 1, 1 - stream] = 1 - chosen if (tick - 1) % 2 else chosen

    def each(at_tick, at_stream, act_on):
        for direction in range(2):

            @pl.when(own_direction(at_tick, at_stream) == direction)
            def _():
                batch = batches[at_tick, at_stream]
                act_on(edges_out[direction], corners_out[direction], batch)

    def old_stores(index, act):
        first, second = older[index]

        def act_on(edges, corners, batch):
            pairs = (
                (first.at[:, :, edge_part], edges.at[0, batch]),
                (second.at[:, :, edge_part], edges.at[1, batch]),
                (second.at[:, :, corner_part], corners.at[batch]),
            )
            for place, (source, target) in enumerate(pairs):
                act(pltpu.make_async_copy(source, target, old_sems.at[index, place]))

        each(tick - 1, histories[index], act_on)

    def tile_store(act, step, at):
        def act_on(edges, corners, batch):
            for slot in range(2):
                act(
                    pltpu.make_async_copy(
                        outs[slot].at[:, :, at], edges.at[slot, batch, :, :, at],
                        sems.at[slot, step],
                    )
                )

        each(tick, stream, act_on)

    def corner_store(act):
        each(
            tick, stream,
            lambda edges, corners, batch: act(
                pltpu.make_async_copy(
                    outs[1].at[:, :, corner_part], corners.at[batch], sems.at[2, 0]
                )
            ),
        )

    for index in range(count):
        old_stores(index, start)
    tiles = []

    def stored(step, at):
        tiles.append((step, at))
        tile_store(start, step, at)

    compute(
        tick, stream, corner_width, first_in, second_in, None, sources, operators, outs, left,
        stored,
    )
    corner_store(start)
    for index in range(count):
        old_stores(index, wait)
    for step, at in tiles:
        tile_store(wait, step, at)
    corner_store(wait)


def tick_shapes(sources, corner_width, tick, ticks, stream):
    _, _, parts, shots, edge_width = sources.shape
    kind = sources.dtype
    first_width = edge_width + (0 if tick == ticks - 1 or tick + stream == 0 else corner_width)
    return [
        pltpu.VMEM((parts, shots, first_width), kind),
        pltpu.VMEM((parts, shots, edge_width + corner_width), kind),
    ]


def cost(flops):
    return pl.CostEstimate(flops=flops, bytes_accessed=1, transcendentals=0)


def left_side(sources):
    _, _, parts, shots, edge_width = sources.shape
    return pltpu.VMEM((2 * parts * shots, 4 * edge_width), sources.dtype)


def middle_tick(
    tick, ticks, stream, first_in, second_in, sources, operators, corner_width, corner_in
):
    shapes = tick_shapes(sources, corner_width, tick, ticks, stream)
    operands = [first_in, second_in, sources, operators]
    if corner_in is not None:
        operands.append(corner_in)
    return pl.pallas_call(
        functools.partial(middle_kernel, tick, stream, corner_width),
        out_shape=shapes,
        in_specs=[VMEM] * len(operands),
        out_specs=[VMEM] * len(shapes),
        scratch_shapes=[left_side(sources)],
        compiler_params=pltpu.CompilerParams(vmem_limit_bytes=VMEM_LIMIT),
        cost_estimate=cost(0 if stream else FIRST if tick == 0 else MIDDLE),
        name="tick" + str(tick) + "_stream" + str(stream),
    )(*operands)


def last_tick(
    tick, ticks, stream, flags, first_in, second_in, sources, operators, history, so_far,
    corner_width,
):
    _, batches, parts, shots, edge_width = sources.shape
    kind = sources.dtype
    outs = [jax.ShapeDtypeStruct((2, batches, parts, shots, edge_width), kind)] * 2
    outs += [jax.ShapeDtypeStruct((batches, parts, shots, corner_width), kind)] * 2
    operands = [flags, first_in, second_in, sources, operators]
    in_specs = [VMEM] * 5
    aliases = {}
    if so_far is None:
        for traces in history:
            operands += list(traces)
        in_specs += [VMEM] * 4
        histories = (0, 1)
    else:
        aliases = {len(operands) + i: i for i in range(4)}
        operands += list(so_far)
        in_specs += [HBM] * 4
        histories = ()
    return pl.pallas_call(
        functools.partial(last_kernel, tick, stream, histories, corner_width),
        out_shape=outs,
        in_specs=in_specs,
        out_specs=[HBM] * 4,
        scratch_shapes=[left_side(sources)]
        + tick_shapes(sources, corner_width, tick, ticks, stream)
        + [pltpu.SemaphoreType.DMA((2, 3)), pltpu.SemaphoreType.DMA((3, 3))],
        input_output_aliases=aliases,
        compiler_params=pltpu.CompilerParams(vmem_limit_bytes=VMEM_LIMIT),
        cost_estimate=cost(0),
        name="tick" + str(tick) + "_stream" + str(stream),
    )(*operands)


def move(array, counts, step_of_cell):
    row_count, col_count = counts
    pairs = []
    for row in range(row_count):
        for col in range(col_count):
            down, right = step_of_cell(row, col)
            to_row = (row + down) % row_count
            to_col = (col + right) % col_count
            pairs.append((row * col_count + col, to_row * col_count + to_col))
    return lax.ppermute(array, ("row", "col"), pairs)


def sense(row, col, tick, stream):
    return -1 if direction_at(row, col, tick, stream) else 1


def by_row(array, counts, tick, stream):
    return move(array, counts, lambda row, col: (sense(row, col, tick - 1, stream), 0))


def by_col(array, counts, tick, stream):
    return move(array, counts, lambda row, col: (0, sense(row, col, tick - 1, stream)))


def by_diagonal(array, counts, stream):
    return move(array, counts, lambda row, col: (sense(row, col, 0, stream),) * 2)


def shards(
    southeast_edges, northwest_edges, southeast_corners, northwest_corners, operators, sources,
    roster,
):
    counts = (lax.axis_size("row"), lax.axis_size("col"))
    ticks = roster.shape[1]
    corner_width = southeast_corners.shape[-1]
    roster = in_hbm(roster.transpose(0, 2, 1))
    states = (
        southeast_edges[0, 0], northwest_edges[0, 0], southeast_corners[0, 0],
        northwest_corners[0, 0],
    )
    slots = [select_initial(counts, 0, roster, states), None]
    *rest, prepared, picked, flags = load_operators(
        counts, 1, roster, states, operators[0, 0], sources[0, 0]
    )
    slots[1] = rest
    corners = [None, None]
    firsts = [slots[stream][0] for stream in range(2)]
    seconds = [slots[stream][1] for stream in range(2)]
    outs = None
    for tick in range(ticks):
        done = []
        for stream in range(2):
            second_in = by_col(seconds[stream], counts, tick, stream)
            if tick == 0:
                corners[stream] = by_diagonal(slots[stream][2], counts, stream)
            first_in = by_row(firsts[stream], counts, tick, stream)
            if tick < ticks - 1:
                corner_in = corners[stream] if tick == 0 else None
                if tick == 1 and stream == 0:
                    corner_in = corners[1]
                done.append(
                    middle_tick(
                        tick, ticks, stream, first_in, second_in, picked, prepared, corner_width,
                        corner_in,
                    )
                )
            else:
                outs = last_tick(
                    tick, ticks, stream, flags, first_in, second_in, picked, prepared, history, outs,
                    corner_width,
                )
        if tick < ticks - 1:
            history = done
            firsts = [done[0][0], done[1][0]]
            seconds = [done[0][1], done[1][1]]
    return tuple(array[None, None] for array in outs)


def solution(mesh):
    edges = P("row", "col", None, None, None, None, None)
    corners = P("row", "col", None, None, None, None)
    return jax.shard_map(
        shards,
        mesh=mesh,
        in_specs=(edges, edges, corners, corners, corners, corners, P()),
        out_specs=(edges, edges, corners, corners),
        check_vma=False,
    )
```

```python
import functools

import jax
import jax.numpy as jnp
from jax import lax
from jax.experimental import pallas as pl
from jax.experimental.pallas import tpu as pltpu
from jax.sharding import PartitionSpec as P

VMEM = pl.BlockSpec(memory_space=pltpu.VMEM)
SMEM = pl.BlockSpec(memory_space=pltpu.SMEM)
HBM = pl.BlockSpec(memory_space=pltpu.HBM)
VMEM_LIMIT = 40 * 1024 * 1024
FIRST = 2000 * 10**6
MIDDLE = 8 * 10**8


def direction_at(row, col, tick, stream):
    return (row + col + tick + 1 + stream) % 2


def in_hbm(array):
    return pltpu.with_memory_space_constraint(array, pltpu.HBM)


def own_direction(tick, stream):
    return direction_at(lax.axis_index("row"), lax.axis_index("col"), tick, stream)


def chosen_at_start(roster_ref, direction, counts):
    row = lax.axis_index("row")
    col = lax.axis_index("col")
    if direction:
        row = counts[0] - 1 - row
        col = counts[1] - 1 - col
    klass = lax.rem(row + col, 2)
    return jnp.where(roster_ref[direction, 0, 0] == klass, 0, 1)


def start(copy):
    copy.start()


def wait(copy):
    copy.wait()


def select_slots(counts, stream, roster, edges, corners, outs, sems, act):
    by_row, by_col, by_diagonal = outs
    edge_width = by_row.shape[-1]
    corner_width = by_diagonal.shape[-1]
    for going in range(2):

        @pl.when(own_direction(-1, stream) == going)
        def _():
            other = 1 - chosen_at_start(roster, going, counts)
            own = going if False else 1 - going
            mine = chosen_at_start(roster, own, counts)
            pairs = (
                (edges[going].at[0, other], by_row),
                (corners[own].at[mine], by_diagonal.at[0]),
                (corners[own].at[1 - mine], by_diagonal.at[1]),
                (edges[going].at[1, other], by_col.at[:, :, pl.ds(0, edge_width)]),
                (corners[going].at[other], by_col.at[:, :, pl.ds(edge_width, corner_width)]),
            )
            for index, (source, target) in enumerate(pairs):
                act(pltpu.make_async_copy(source, target, sems.at[index]))


def select_kernel(
    counts, stream, roster, se_edges, nw_edges, se_corners, nw_corners, by_row, by_col, by_diagonal,
    numbers, all_edges, all_corners, sems
):
    edges, corners = (se_edges, nw_edges), (se_corners, nw_corners)
    roster_copy = pltpu.make_async_copy(roster, numbers, sems.at[0])
    roster_copy.start()
    own = 1 - own_direction(-1, stream)

    def fetch(act):
        for going in range(2):

            @pl.when(own_direction(-1, stream) == going)
            def _():
                act(pltpu.make_async_copy(edges[going], all_edges, sems.at[1]))
                act(pltpu.make_async_copy(corners[1 - going], all_corners, sems.at[2]))

    fetch(start)
    roster_copy.wait()
    chosen = [chosen_at_start(numbers, direction, counts) for direction in range(2)]
    other = 1 - jnp.where(own == 0, chosen[1], chosen[0])
    mine = jnp.where(own == 0, chosen[0], chosen[1])
    fetch(wait)
    by_row[...] = all_edges[0, other]
    by_col[...] = all_edges[1, other]
    by_diagonal[...] = all_corners[mine]


def slot_shapes(edges, corners, late):
    _, _, parts, shots, edge_width = edges.shape
    corner_width = corners.shape[-1]
    kind = edges.dtype
    return [
        pltpu.VMEM((parts, shots, edge_width), kind),
        pltpu.VMEM((parts, shots, edge_width + (corner_width if late else 0)), kind),
        pltpu.VMEM(((2,) if late else ()) + (parts, shots, corner_width), kind),
    ]


def select_initial(counts, stream, roster, states):
    edges, _, corners, _ = states
    return pl.pallas_call(
        functools.partial(select_kernel, counts, stream),
        out_shape=slot_shapes(edges, corners, False),
        in_specs=[HBM] * 5,
        out_specs=[VMEM] * 3,
        scratch_shapes=[
            pltpu.SMEM(roster.shape, roster.dtype),
            pltpu.VMEM(edges.shape, edges.dtype),
            pltpu.VMEM(corners.shape, corners.dtype),
            pltpu.SemaphoreType.DMA((3,)),
        ],
        compiler_params=pltpu.CompilerParams(vmem_limit_bytes=VMEM_LIMIT),
        name="select_initial",
    )(roster, *map(in_hbm, states))


def load_kernel(
    counts, stream, roster, se_edges, nw_edges, se_corners, nw_corners, operators, sources, *refs
):
    outs = refs[:3]
    prepared, picked, flags, select_sems, operator_sems, source_sems = refs[3:]
    count, edge_width, _ = operators.shape
    copies = [
        pltpu.make_async_copy(
            operators.at[i],
            prepared.at[0, pl.ds(i * edge_width, edge_width)],
            operator_sems.at[i],
        )
        for i in range(count)
    ]
    source_copies = []
    for direction in range(2):
        mine = chosen_at_start(roster, direction, counts)
        flags[direction] = jnp.full(flags.shape[1:], mine.astype(jnp.float32))
        for late in range(2):
            source_copies.append(
                pltpu.make_async_copy(
                    sources.at[1 - mine if late else mine],
                    picked.at[direction, late],
                    source_sems.at[direction, late],
                )
            )
    edges, corners = (se_edges, nw_edges), (se_corners, nw_corners)
    for copy in copies:
        copy.start()
    select_slots(counts, stream, roster, edges, corners, outs, select_sems, start)
    for copy in source_copies:
        copy.start()
    for i in range(count):
        copies[i].wait()
        rows = pl.ds(i * edge_width, edge_width)
        prepared[1, rows, :] = prepared[0, rows, :].T
    select_slots(counts, stream, roster, edges, corners, outs, select_sems, wait)
    for copy in source_copies:
        copy.wait()


def load_operators(counts, stream, roster, states, operators, sources):
    count = operators.shape[0] * operators.shape[1]
    edge_width = operators.shape[-1]
    kind = operators.dtype
    operators = operators.reshape(count, edge_width, edge_width)
    return pl.pallas_call(
        functools.partial(load_kernel, counts, stream),
        out_shape=slot_shapes(states[0], states[2], True)
        + [
            pltpu.VMEM((2, count * edge_width, edge_width), kind),
            pltpu.VMEM((2,) + sources.shape, kind),
            pltpu.VMEM((2, 8, 128), jnp.float32),
        ],
        in_specs=[SMEM] + [HBM] * 6,
        out_specs=[VMEM] * 6,
        scratch_shapes=[
            pltpu.SemaphoreType.DMA((5,)),
            pltpu.SemaphoreType.DMA((count,)),
            pltpu.SemaphoreType.DMA((2, 2)),
        ],
        compiler_params=pltpu.CompilerParams(vmem_limit_bytes=VMEM_LIMIT),
        cost_estimate=cost(0),
        name="load_operators",
    )(roster, *map(in_hbm, states), in_hbm(operators), in_hbm(sources))


def compute(
    tick, stream, corner_width, first_in, second_in, corner_in, sources, operators, outs, left, act
):
    first_out, second_out = outs
    parts, shots, edge_width = sources.shape[2:]
    rows = parts * shots
    direction = own_direction(tick, stream)
    edge_part = pl.ds(0, edge_width)
    corner_part = pl.ds(edge_width, corner_width)

    for place, ref in ((0, first_in), (2, second_in)):
        other_place = 2 - place
        real = ref[0, :, edge_part]
        imag = ref[1, :, edge_part]
        minus = -imag
        for slot, block in ((place, 0), (other_place, 1)):
            row = block * rows
            column = slot * edge_width
            left[pl.ds(row, shots), pl.ds(column, edge_width)] = real
            left[pl.ds(row + shots, shots), pl.ds(column, edge_width)] = imag
            left[pl.ds(row, shots), pl.ds(column + edge_width, edge_width)] = minus
            left[pl.ds(row + shots, shots), pl.ds(column + edge_width, edge_width)] = real

    if corner_in is None:
        corner = first_in[:, :, corner_part]
    else:
        corner = corner_in[...] if len(corner_in.shape) == 3 else corner_in[tick]
    corner = corner.astype(jnp.float32).reshape(rows, corner_width)
    if first_out.shape[-1] > edge_width:
        first_out[:, :, corner_part] = second_in[:, :, corner_part]

    tile = edge_width // 3 if edge_width % 3 == 0 else edge_width
    steps = edge_width // tile
    for step in range(steps):
        at = pl.ds(step * tile, tile)
        value = jnp.dot(left[...], operators[direction, :, at], preferred_element_type=jnp.float32)
        source = sources[direction, tick % 2, :, :, at].astype(jnp.float32).reshape(rows, tile)
        first = value[:rows] + source
        second = value[rows:] + source
        for end in range(2):
            if step != (steps - 1 if end else 0):
                continue
            here = slice(tile - corner_width, tile) if end else slice(0, corner_width)
            added = jnp.where(direction == end, corner, 0.0)
            widths = ((0, 0), (tile - corner_width, 0) if end else (0, tile - corner_width))
            added = jnp.pad(added, widths)
            first = first + added
            second = second + added
            given = (0.5 * (first[:, here] + second[:, here])).astype(second_out.dtype)
            given = given.reshape(parts, shots, corner_width)

            @pl.when(direction != end)
            def _():
                second_out[:, :, corner_part] = given

        first_out[:, :, at] = first.astype(first_out.dtype).reshape(parts, shots, tile)
        second_out[:, :, at] = second.astype(second_out.dtype).reshape(parts, shots, tile)
        act(step, at)


def in_order(stream, first, second):
    return (second, first) if stream else (first, second)


def middle_kernel(
    tick, stream, corner_width, first_in, second_in, sources, operators, *refs
):
    *corner_in, first_out, second_out, left = refs
    outs = (first_out, second_out)
    corner_in = corner_in[0] if corner_in else None
    compute(
        tick, stream, corner_width, first_in, second_in, corner_in, sources, operators, outs, left,
        lambda step, at: None,
    )


def last_kernel(
    tick, stream, histories, corner_width, flags, one_in, two_in, sources, operators, *refs
):
    first_in, second_in = in_order(stream, one_in, two_in)
    count = len(histories)
    older = [refs[2 * i : 2 * i + 2] for i in range(count)]
    refs = refs[2 * count :]
    if not count:
        refs = refs[4:]
    edges_out, corners_out, (left, *outs, old_sems, sems) = refs[0:2], refs[2:4], refs[4:]
    edge_width = sources.shape[-1]
    edge_part = pl.ds(0, edge_width)
    corner_part = pl.ds(edge_width, corner_width)

    batches = {}
    for at_tick in (tick - 1, tick) if count else (tick,):
        chosen = jnp.max(flags[own_direction(at_tick, stream), :1]).astype(jnp.int32)
        batches[at_tick, stream] = 1 - chosen if at_tick % 2 else chosen
    if count:
        chosen = jnp.max(flags[own_direction(tick - 1, 1 - stream), :1]).astype(jnp.int32)
        batches[tick - 1, 1 - stream] = 1 - chosen if (tick - 1) % 2 else chosen

    def each(at_tick, at_stream, act_on):
        for direction in range(2):

            @pl.when(own_direction(at_tick, at_stream) == direction)
            def _():
                batch = batches[at_tick, at_stream]
                act_on(edges_out[direction], corners_out[direction], batch)

    def old_stores(index, act):
        first, second = older[index]

        def act_on(edges, corners, batch):
            pairs = (
                (first.at[:, :, edge_part], edges.at[0, batch]),
                (second.at[:, :, edge_part], edges.at[1, batch]),
                (second.at[:, :, corner_part], corners.at[batch]),
            )
            for place, (source, target) in enumerate(pairs):
                act(pltpu.make_async_copy(source, target, old_sems.at[index, place]))

        each(tick - 1, histories[index], act_on)

    def tile_store(act, step, at):
        def act_on(edges, corners, batch):
            for slot in range(2):
                act(
                    pltpu.make_async_copy(
                        outs[slot].at[:, :, at], edges.at[slot, batch, :, :, at],
                        sems.at[slot, step],
                    )
                )

        each(tick, stream, act_on)

    def corner_store(act):
        each(
            tick, stream,
            lambda edges, corners, batch: act(
                pltpu.make_async_copy(
                    outs[1].at[:, :, corner_part], corners.at[batch], sems.at[2, 0]
                )
            ),
        )

    for index in range(count):
        old_stores(index, start)
    tiles = []

    def stored(step, at):
        tiles.append((step, at))
        tile_store(start, step, at)

    compute(
        tick, stream, corner_width, first_in, second_in, None, sources, operators, outs, left,
        stored,
    )
    corner_store(start)
    for index in range(count):
        old_stores(index, wait)
    for step, at in tiles:
        tile_store(wait, step, at)
    corner_store(wait)


def tick_shapes(sources, corner_width, tick, ticks, stream):
    _, _, parts, shots, edge_width = sources.shape
    kind = sources.dtype
    first_width = edge_width + (0 if tick == ticks - 1 or tick + stream == 0 else corner_width)
    return [
        pltpu.VMEM((parts, shots, first_width), kind),
        pltpu.VMEM((parts, shots, edge_width + corner_width), kind),
    ]


def cost(flops):
    return pl.CostEstimate(flops=flops, bytes_accessed=1, transcendentals=0)


def left_side(sources):
    _, _, parts, shots, edge_width = sources.shape
    return pltpu.VMEM((2 * parts * shots, 4 * edge_width), sources.dtype)


def middle_tick(
    tick, ticks, stream, first_in, second_in, sources, operators, corner_width, corner_in
):
    shapes = tick_shapes(sources, corner_width, tick, ticks, stream)
    operands = [first_in, second_in, sources, operators]
    if corner_in is not None:
        operands.append(corner_in)
    return pl.pallas_call(
        functools.partial(middle_kernel, tick, stream, corner_width),
        out_shape=shapes,
        in_specs=[VMEM] * len(operands),
        out_specs=[VMEM] * len(shapes),
        scratch_shapes=[left_side(sources)],
        compiler_params=pltpu.CompilerParams(vmem_limit_bytes=VMEM_LIMIT),
        cost_estimate=cost(0 if stream else FIRST if tick == 0 else MIDDLE),
        name="tick" + str(tick) + "_stream" + str(stream),
    )(*operands)


def last_tick(
    tick, ticks, stream, flags, first_in, second_in, sources, operators, history, so_far,
    corner_width,
):
    _, batches, parts, shots, edge_width = sources.shape
    kind = sources.dtype
    outs = [jax.ShapeDtypeStruct((2, batches, parts, shots, edge_width), kind)] * 2
    outs += [jax.ShapeDtypeStruct((batches, parts, shots, corner_width), kind)] * 2
    operands = [flags, *in_order(stream, first_in, second_in), sources, operators]
    in_specs = [VMEM] * 5
    aliases = {}
    if so_far is None:
        for traces in history:
            operands += list(traces)
        in_specs += [VMEM] * 4
        histories = (0, 1)
    else:
        aliases = {len(operands) + i: i for i in range(4)}
        operands += list(so_far)
        in_specs += [HBM] * 4
        histories = ()
    return pl.pallas_call(
        functools.partial(last_kernel, tick, stream, histories, corner_width),
        out_shape=outs,
        in_specs=in_specs,
        out_specs=[HBM] * 4,
        scratch_shapes=[left_side(sources)]
        + tick_shapes(sources, corner_width, tick, ticks, stream)
        + [pltpu.SemaphoreType.DMA((2, 3)), pltpu.SemaphoreType.DMA((3, 3))],
        input_output_aliases=aliases,
        compiler_params=pltpu.CompilerParams(vmem_limit_bytes=VMEM_LIMIT),
        cost_estimate=cost(0),
        name="tick" + str(tick) + "_stream" + str(stream),
    )(*operands)


def move(array, counts, step_of_cell):
    row_count, col_count = counts
    pairs = []
    for row in range(row_count):
        for col in range(col_count):
            down, right = step_of_cell(row, col)
            to_row = (row + down) % row_count
            to_col = (col + right) % col_count
            pairs.append((row * col_count + col, to_row * col_count + to_col))
    return lax.ppermute(array, ("row", "col"), pairs)


def sense(row, col, tick, stream):
    return -1 if direction_at(row, col, tick, stream) else 1


def by_row(array, counts, tick, stream):
    return move(array, counts, lambda row, col: (sense(row, col, tick - 1, stream), 0))


def by_col(array, counts, tick, stream):
    return move(array, counts, lambda row, col: (0, sense(row, col, tick - 1, stream)))


def by_diagonal(array, counts, stream):
    return move(array, counts, lambda row, col: (sense(row, col, 0, stream),) * 2)


def shards(
    southeast_edges, northwest_edges, southeast_corners, northwest_corners, operators, sources,
    roster,
):
    counts = (lax.axis_size("row"), lax.axis_size("col"))
    ticks = roster.shape[1]
    corner_width = southeast_corners.shape[-1]
    roster = in_hbm(roster.transpose(0, 2, 1))
    states = (
        southeast_edges[0, 0], northwest_edges[0, 0], southeast_corners[0, 0],
        northwest_corners[0, 0],
    )
    slots = [select_initial(counts, 0, roster, states), None]
    *rest, prepared, picked, flags = load_operators(
        counts, 1, roster, states, operators[0, 0], sources[0, 0]
    )
    slots[1] = rest
    corners = [None, None]
    firsts = [slots[stream][0] for stream in range(2)]
    seconds = [slots[stream][1] for stream in range(2)]
    outs = None
    for tick in range(ticks):
        done = []
        for stream in range(2):
            second_in = by_col(seconds[stream], counts, tick, stream)
            if tick == 0:
                corners[stream] = by_diagonal(slots[stream][2], counts, stream)
            first_in = by_row(firsts[stream], counts, tick, stream)
            if tick < ticks - 1:
                corner_in = corners[stream] if tick == 0 else None
                if tick == 1 and stream == 0:
                    corner_in = corners[1]
                done.append(
                    middle_tick(
                        tick, ticks, stream, first_in, second_in, picked, prepared, corner_width,
                        corner_in,
                    )
                )
            else:
                outs = last_tick(
                    tick, ticks, stream, flags, first_in, second_in, picked, prepared, history, outs,
                    corner_width,
                )
        if tick < ticks - 1:
            history = done
            firsts = [done[0][0], done[1][0]]
            seconds = [done[0][1], done[1][1]]
    return tuple(array[None, None] for array in outs)


def solution(mesh):
    edges = P("row", "col", None, None, None, None, None)
    corners = P("row", "col", None, None, None, None)
    return jax.shard_map(
        shards,
        mesh=mesh,
        in_specs=(edges, edges, corners, corners, corners, corners, P()),
        out_specs=(edges, edges, corners, corners),
        check_vma=False,
    )
```

```python
import functools

import jax
import jax.numpy as jnp
from jax import lax
from jax.experimental import pallas as pl
from jax.experimental.pallas import tpu as pltpu
from jax.sharding import PartitionSpec as P

VMEM = pl.BlockSpec(memory_space=pltpu.VMEM)
SMEM = pl.BlockSpec(memory_space=pltpu.SMEM)
HBM = pl.BlockSpec(memory_space=pltpu.HBM)
VMEM_LIMIT = 40 * 1024 * 1024
FIRST = 2000 * 10**6
MIDDLE = 8 * 10**8


def direction_at(row, col, tick, stream):
    return (row + col + tick + 1 + stream) % 2


def in_hbm(array):
    return pltpu.with_memory_space_constraint(array, pltpu.HBM)


def own_direction(tick, stream):
    return direction_at(lax.axis_index("row"), lax.axis_index("col"), tick, stream)


def chosen_at_start(roster_ref, direction, counts):
    row = lax.axis_index("row")
    col = lax.axis_index("col")
    if direction:
        row = counts[0] - 1 - row
        col = counts[1] - 1 - col
    klass = lax.rem(row + col, 2)
    return jnp.where(roster_ref[direction, 0, 0] == klass, 0, 1)


def start(copy):
    copy.start()


def wait(copy):
    copy.wait()


def select_slots(counts, stream, roster, edges, corners, outs, sems, act):
    by_row, by_col, by_diagonal = outs
    edge_width = by_row.shape[-1]
    corner_width = by_diagonal.shape[-1]
    for going in range(2):

        @pl.when(own_direction(-1, stream) == going)
        def _():
            other = 1 - chosen_at_start(roster, going, counts)
            own = going if False else 1 - going
            mine = chosen_at_start(roster, own, counts)
            pairs = (
                (edges[going].at[0, other], by_row),
                (corners[own].at[mine], by_diagonal.at[0]),
                (corners[own].at[1 - mine], by_diagonal.at[1]),
                (edges[going].at[1, other], by_col.at[:, :, pl.ds(0, edge_width)]),
                (corners[going].at[other], by_col.at[:, :, pl.ds(edge_width, corner_width)]),
            )
            for index, (source, target) in enumerate(pairs):
                act(pltpu.make_async_copy(source, target, sems.at[index]))


def select_kernel(
    counts, stream, roster, se_edges, nw_edges, se_corners, nw_corners, by_row, by_col, by_diagonal,
    numbers, all_edges, all_corners, sems
):
    edges, corners = (se_edges, nw_edges), (se_corners, nw_corners)
    roster_copy = pltpu.make_async_copy(roster, numbers, sems.at[0])
    roster_copy.start()
    own = 1 - own_direction(-1, stream)

    def fetch(act):
        for going in range(2):

            @pl.when(own_direction(-1, stream) == going)
            def _():
                act(pltpu.make_async_copy(edges[going], all_edges, sems.at[1]))
                act(pltpu.make_async_copy(corners[1 - going], all_corners, sems.at[2]))

    fetch(start)
    roster_copy.wait()
    chosen = [chosen_at_start(numbers, direction, counts) for direction in range(2)]
    other = 1 - jnp.where(own == 0, chosen[1], chosen[0])
    mine = jnp.where(own == 0, chosen[0], chosen[1])
    fetch(wait)
    by_row[...] = all_edges[0, other]
    by_col[...] = all_edges[1, other]
    by_diagonal[...] = all_corners[mine]


def slot_shapes(edges, corners, late):
    _, _, parts, shots, edge_width = edges.shape
    corner_width = corners.shape[-1]
    kind = edges.dtype
    return [
        pltpu.VMEM((parts, shots, edge_width), kind),
        pltpu.VMEM((parts, shots, edge_width + (corner_width if late else 0)), kind),
        pltpu.VMEM(((2,) if late else ()) + (parts, shots, corner_width), kind),
    ]


def select_initial(counts, stream, roster, states):
    edges, _, corners, _ = states
    return pl.pallas_call(
        functools.partial(select_kernel, counts, stream),
        out_shape=slot_shapes(edges, corners, False),
        in_specs=[HBM] * 5,
        out_specs=[VMEM] * 3,
        scratch_shapes=[
            pltpu.SMEM(roster.shape, roster.dtype),
            pltpu.VMEM(edges.shape, edges.dtype),
            pltpu.VMEM(corners.shape, corners.dtype),
            pltpu.SemaphoreType.DMA((3,)),
        ],
        compiler_params=pltpu.CompilerParams(vmem_limit_bytes=VMEM_LIMIT),
        name="select_initial",
    )(roster, *map(in_hbm, states))


def load_kernel(
    counts, stream, roster, se_edges, nw_edges, se_corners, nw_corners, operators, sources, *refs
):
    outs = refs[:3]
    prepared, picked, flags, select_sems, operator_sems, source_sems = refs[3:]
    count, edge_width, _ = operators.shape
    copies = [
        pltpu.make_async_copy(
            operators.at[i],
            prepared.at[0, pl.ds(i * edge_width, edge_width)],
            operator_sems.at[i],
        )
        for i in range(count)
    ]
    source_copies = []
    for direction in range(2):
        mine = chosen_at_start(roster, direction, counts)
        flags[direction] = jnp.full(flags.shape[1:], mine.astype(jnp.float32))
        for late in range(2):
            source_copies.append(
                pltpu.make_async_copy(
                    sources.at[1 - mine if late else mine],
                    picked.at[direction, late],
                    source_sems.at[direction, late],
                )
            )
    edges, corners = (se_edges, nw_edges), (se_corners, nw_corners)
    for copy in copies:
        copy.start()
    select_slots(counts, stream, roster, edges, corners, outs, select_sems, start)
    for copy in source_copies:
        copy.start()
    for i in range(count):
        copies[i].wait()
        rows = pl.ds(i * edge_width, edge_width)
        prepared[1, rows, :] = prepared[0, rows, :].T
    select_slots(counts, stream, roster, edges, corners, outs, select_sems, wait)
    for copy in source_copies:
        copy.wait()


def load_operators(counts, stream, roster, states, operators, sources):
    count = operators.shape[0] * operators.shape[1]
    edge_width = operators.shape[-1]
    kind = operators.dtype
    operators = operators.reshape(count, edge_width, edge_width)
    return pl.pallas_call(
        functools.partial(load_kernel, counts, stream),
        out_shape=slot_shapes(states[0], states[2], True)
        + [
            pltpu.VMEM((2, count * edge_width, edge_width), kind),
            pltpu.VMEM((2,) + sources.shape, kind),
            pltpu.VMEM((2, 8, 128), jnp.float32),
        ],
        in_specs=[SMEM] + [HBM] * 6,
        out_specs=[VMEM] * 6,
        scratch_shapes=[
            pltpu.SemaphoreType.DMA((5,)),
            pltpu.SemaphoreType.DMA((count,)),
            pltpu.SemaphoreType.DMA((2, 2)),
        ],
        compiler_params=pltpu.CompilerParams(vmem_limit_bytes=VMEM_LIMIT),
        cost_estimate=cost(0),
        name="load_operators",
    )(roster, *map(in_hbm, states), in_hbm(operators), in_hbm(sources))


def compute(
    tick, stream, corner_width, first_in, second_in, corner_in, sources, operators, outs, left, act
):
    first_out, second_out = outs
    parts, shots, edge_width = sources.shape[2:]
    rows = parts * shots
    direction = own_direction(tick, stream)
    edge_part = pl.ds(0, edge_width)
    corner_part = pl.ds(edge_width, corner_width)

    for place, ref in ((0, first_in), (2, second_in)):
        other_place = 2 - place
        real = ref[0, :, edge_part]
        imag = ref[1, :, edge_part]
        minus = -imag
        for slot, block in ((place, 0), (other_place, 1)):
            row = block * rows
            column = slot * edge_width
            left[pl.ds(row, shots), pl.ds(column, edge_width)] = real
            left[pl.ds(row + shots, shots), pl.ds(column, edge_width)] = imag
            left[pl.ds(row, shots), pl.ds(column + edge_width, edge_width)] = minus
            left[pl.ds(row + shots, shots), pl.ds(column + edge_width, edge_width)] = real

    if corner_in is None:
        corner = first_in[:, :, corner_part]
    else:
        corner = corner_in[...] if len(corner_in.shape) == 3 else corner_in[tick]
    corner = corner.astype(jnp.float32).reshape(rows, corner_width)
    if first_out.shape[-1] > edge_width:
        first_out[:, :, corner_part] = second_in[:, :, corner_part]

    tile = edge_width // 3 if edge_width % 3 == 0 else edge_width
    steps = edge_width // tile
    for step in range(steps):
        at = pl.ds(step * tile, tile)
        value = jnp.dot(left[...], operators[direction, :, at], preferred_element_type=jnp.float32)
        source = sources[direction, tick % 2, :, :, at].astype(jnp.float32).reshape(rows, tile)
        first = value[:rows] + source
        second = value[rows:] + source
        for end in range(2):
            if step != (steps - 1 if end else 0):
                continue
            here = slice(tile - corner_width, tile) if end else slice(0, corner_width)
            added = jnp.where(direction == end, corner, 0.0)
            widths = ((0, 0), (tile - corner_width, 0) if end else (0, tile - corner_width))
            added = jnp.pad(added, widths)
            first = first + added
            second = second + added
            given = (0.5 * (first[:, here] + second[:, here])).astype(second_out.dtype)
            given = given.reshape(parts, shots, corner_width)

            @pl.when(direction != end)
            def _():
                second_out[:, :, corner_part] = given

        first_out[:, :, at] = first.astype(first_out.dtype).reshape(parts, shots, tile)
        second_out[:, :, at] = second.astype(second_out.dtype).reshape(parts, shots, tile)
        act(step, at)


def in_order(stream, first, second):
    return (second, first) if stream else (first, second)


def middle_kernel(
    tick, stream, corner_width, one_in, two_in, sources, operators, *refs
):
    first_in, second_in = in_order(tick * stream, one_in, two_in)
    *corner_in, first_out, second_out, left = refs
    outs = (first_out, second_out)
    corner_in = corner_in[0] if corner_in else None
    compute(
        tick, stream, corner_width, first_in, second_in, corner_in, sources, operators, outs, left,
        lambda step, at: None,
    )


def last_kernel(
    tick, stream, histories, corner_width, flags, one_in, two_in, sources, operators, *refs
):
    first_in, second_in = in_order(stream, one_in, two_in)
    count = len(histories)
    older = [refs[2 * i : 2 * i + 2] for i in range(count)]
    refs = refs[2 * count :]
    if not count:
        refs = refs[4:]
    edges_out, corners_out, (left, *outs, old_sems, sems) = refs[0:2], refs[2:4], refs[4:]
    edge_width = sources.shape[-1]
    edge_part = pl.ds(0, edge_width)
    corner_part = pl.ds(edge_width, corner_width)

    batches = {}
    for at_tick in (tick - 1, tick) if count else (tick,):
        chosen = jnp.max(flags[own_direction(at_tick, stream), :1]).astype(jnp.int32)
        batches[at_tick, stream] = 1 - chosen if at_tick % 2 else chosen
    if count:
        chosen = jnp.max(flags[own_direction(tick - 1, 1 - stream), :1]).astype(jnp.int32)
        batches[tick - 1, 1 - stream] = 1 - chosen if (tick - 1) % 2 else chosen

    def each(at_tick, at_stream, act_on):
        for direction in range(2):

            @pl.when(own_direction(at_tick, at_stream) == direction)
            def _():
                batch = batches[at_tick, at_stream]
                act_on(edges_out[direction], corners_out[direction], batch)

    def old_stores(index, act):
        first, second = older[index]

        def act_on(edges, corners, batch):
            pairs = (
                (first.at[:, :, edge_part], edges.at[0, batch]),
                (second.at[:, :, edge_part], edges.at[1, batch]),
                (second.at[:, :, corner_part], corners.at[batch]),
            )
            for place, (source, target) in enumerate(pairs):
                act(pltpu.make_async_copy(source, target, old_sems.at[index, place]))

        each(tick - 1, histories[index], act_on)

    def tile_store(act, step, at):
        def act_on(edges, corners, batch):
            for slot in range(2):
                act(
                    pltpu.make_async_copy(
                        outs[slot].at[:, :, at], edges.at[slot, batch, :, :, at],
                        sems.at[slot, step],
                    )
                )

        each(tick, stream, act_on)

    def corner_store(act):
        each(
            tick, stream,
            lambda edges, corners, batch: act(
                pltpu.make_async_copy(
                    outs[1].at[:, :, corner_part], corners.at[batch], sems.at[2, 0]
                )
            ),
        )

    for index in range(count):
        old_stores(index, start)
    tiles = []

    def stored(step, at):
        tiles.append((step, at))
        tile_store(start, step, at)

    compute(
        tick, stream, corner_width, first_in, second_in, None, sources, operators, outs, left,
        stored,
    )
    corner_store(start)
    for index in range(count):
        old_stores(index, wait)
    for step, at in tiles:
        tile_store(wait, step, at)
    corner_store(wait)


def tick_shapes(sources, corner_width, tick, ticks, stream):
    _, _, parts, shots, edge_width = sources.shape
    kind = sources.dtype
    first_width = edge_width + (0 if tick == ticks - 1 or tick + stream == 0 else corner_width)
    return [
        pltpu.VMEM((parts, shots, first_width), kind),
        pltpu.VMEM((parts, shots, edge_width + corner_width), kind),
    ]


def cost(flops):
    return pl.CostEstimate(flops=flops, bytes_accessed=1, transcendentals=0)


def left_side(sources):
    _, _, parts, shots, edge_width = sources.shape
    return pltpu.VMEM((2 * parts * shots, 4 * edge_width), sources.dtype)


def middle_tick(
    tick, ticks, stream, first_in, second_in, sources, operators, corner_width, corner_in
):
    shapes = tick_shapes(sources, corner_width, tick, ticks, stream)
    operands = [*in_order(tick * stream, first_in, second_in), sources, operators]
    if corner_in is not None:
        operands.append(corner_in)
    return pl.pallas_call(
        functools.partial(middle_kernel, tick, stream, corner_width),
        out_shape=shapes,
        in_specs=[VMEM] * len(operands),
        out_specs=[VMEM] * len(shapes),
        scratch_shapes=[left_side(sources)],
        compiler_params=pltpu.CompilerParams(vmem_limit_bytes=VMEM_LIMIT),
        cost_estimate=cost(0 if stream else FIRST if tick == 0 else MIDDLE),
        name="tick" + str(tick) + "_stream" + str(stream),
    )(*operands)


def last_tick(
    tick, ticks, stream, flags, first_in, second_in, sources, operators, history, so_far,
    corner_width,
):
    _, batches, parts, shots, edge_width = sources.shape
    kind = sources.dtype
    outs = [jax.ShapeDtypeStruct((2, batches, parts, shots, edge_width), kind)] * 2
    outs += [jax.ShapeDtypeStruct((batches, parts, shots, corner_width), kind)] * 2
    operands = [flags, *in_order(stream, first_in, second_in), sources, operators]
    in_specs = [VMEM] * 5
    aliases = {}
    if so_far is None:
        for traces in history:
            operands += list(traces)
        in_specs += [VMEM] * 4
        histories = (0, 1)
    else:
        aliases = {len(operands) + i: i for i in range(4)}
        operands += list(so_far)
        in_specs += [HBM] * 4
        histories = ()
    return pl.pallas_call(
        functools.partial(last_kernel, tick, stream, histories, corner_width),
        out_shape=outs,
        in_specs=in_specs,
        out_specs=[HBM] * 4,
        scratch_shapes=[left_side(sources)]
        + tick_shapes(sources, corner_width, tick, ticks, stream)
        + [pltpu.SemaphoreType.DMA((2, 3)), pltpu.SemaphoreType.DMA((3, 3))],
        input_output_aliases=aliases,
        compiler_params=pltpu.CompilerParams(vmem_limit_bytes=VMEM_LIMIT),
        cost_estimate=cost(0),
        name="tick" + str(tick) + "_stream" + str(stream),
    )(*operands)


def move(array, counts, step_of_cell):
    row_count, col_count = counts
    pairs = []
    for row in range(row_count):
        for col in range(col_count):
            down, right = step_of_cell(row, col)
            to_row = (row + down) % row_count
            to_col = (col + right) % col_count
            pairs.append((row * col_count + col, to_row * col_count + to_col))
    return lax.ppermute(array, ("row", "col"), pairs)


def sense(row, col, tick, stream):
    return -1 if direction_at(row, col, tick, stream) else 1


def by_row(array, counts, tick, stream):
    return move(array, counts, lambda row, col: (sense(row, col, tick - 1, stream), 0))


def by_col(array, counts, tick, stream):
    return move(array, counts, lambda row, col: (0, sense(row, col, tick - 1, stream)))


def by_diagonal(array, counts, stream):
    return move(array, counts, lambda row, col: (sense(row, col, 0, stream),) * 2)


def shards(
    southeast_edges, northwest_edges, southeast_corners, northwest_corners, operators, sources,
    roster,
):
    counts = (lax.axis_size("row"), lax.axis_size("col"))
    ticks = roster.shape[1]
    corner_width = southeast_corners.shape[-1]
    roster = in_hbm(roster.transpose(0, 2, 1))
    states = (
        southeast_edges[0, 0], northwest_edges[0, 0], southeast_corners[0, 0],
        northwest_corners[0, 0],
    )
    slots = [select_initial(counts, 0, roster, states), None]
    *rest, prepared, picked, flags = load_operators(
        counts, 1, roster, states, operators[0, 0], sources[0, 0]
    )
    slots[1] = rest
    corners = [None, None]
    firsts = [slots[stream][0] for stream in range(2)]
    seconds = [slots[stream][1] for stream in range(2)]
    outs = None
    for tick in range(ticks):
        done = []
        for stream in range(2):
            second_in = by_col(seconds[stream], counts, tick, stream)
            if tick == 0:
                corners[stream] = by_diagonal(slots[stream][2], counts, stream)
            first_in = by_row(firsts[stream], counts, tick, stream)
            if tick < ticks - 1:
                corner_in = corners[stream] if tick == 0 else None
                if tick == 1 and stream == 0:
                    corner_in = corners[1]
                done.append(
                    middle_tick(
                        tick, ticks, stream, first_in, second_in, picked, prepared, corner_width,
                        corner_in,
                    )
                )
            else:
                outs = last_tick(
                    tick, ticks, stream, flags, first_in, second_in, picked, prepared, history, outs,
                    corner_width,
                )
        if tick < ticks - 1:
            history = done
            firsts = [done[0][0], done[1][0]]
            seconds = [done[0][1], done[1][1]]
    return tuple(array[None, None] for array in outs)


def solution(mesh):
    edges = P("row", "col", None, None, None, None, None)
    corners = P("row", "col", None, None, None, None)
    return jax.shard_map(
        shards,
        mesh=mesh,
        in_specs=(edges, edges, corners, corners, corners, corners, P()),
        out_specs=(edges, edges, corners, corners),
        check_vma=False,
    )
```
